512 devices in a mesh: ctx: 16 (over y, core), ch: 32 (over z, x).
Axes of the slice: x: 4, y: 8, z: 8, core: 2. Of those that a mesh axis runs over, the one named last changes fastest.
Arguments:
- records: bfloat16 [8192, 3, 4096], P(('ctx', 'ch')), may hold values from -6 to 6
- rec_slot: int32 [16, 32], replicated, may hold values from 0 to 31, as said below
- short_w: float32 [3, 4096, 3], P(None, 'ch'), may hold values from -3 to 3
- residue: float32 [4096, 16], P('ch'), may hold values from -5 to 5
- rate: float32 [4096, 16], P('ch'), may hold values from 6.1035156e-05 to 0.03
- passthrough: float32 [4096], P('ch'), may hold values from -4 to 4
Outputs:
- gated_out: bfloat16 [8192, 4096], P('ctx', 'ch')
The draws below stay inside these ranges and needn't reach their ends.
Inputs may be any that keep to these rules, and one draw needn't show every extreme that they name: Record r entering along ctx index s goes to ctx index r mod 16; there rec_slot[s, r] is its record slot, and the records reaching one index take each slot 0 to 31 exactly once.
All inputs are finite; a program needn't handle non-finite values.
Results may differ from the reference program's by a relative error of at most 0.008.
Values may be sent and summed in bfloat16 or wider, within the bound.
A program may use at most 64 MiB of HBM per device.

```python
import math
import jax
import jax.numpy as jnp
from jax import lax

CH = 4096
MODES = 16
TOKENS = 8192
RECS = 32
BLOCK = 16
N_CTX = 16


def draw_rec_slot(key, part):
    key = jax.random.fold_in(key, 7)
    sub_keys = jax.random.split(key, N_CTX)
    orders = jax.vmap(lambda sub_key: jax.random.permutation(sub_key, RECS))(sub_keys)
    source = jnp.arange(N_CTX, dtype=jnp.int32)[:, None]
    record = jnp.arange(RECS, dtype=jnp.int32)[None, :]
    per_group = RECS // N_CTX
    return orders[record % N_CTX, source * per_group + record // N_CTX].astype(jnp.int32)


def level_of(own_key, extent, shards, smallest, top_value):
    gain, own = 1.0, jax.random.fold_in(own_key, 6)
    for position, blocks in shards:
        steps = jnp.exp(jax.random.uniform(jax.random.fold_in(own, position), (blocks,), jnp.float32, smallest / len(shards), top_value / len(shards)))
        gain = gain * jnp.repeat(steps, extent[position] // blocks).reshape([-1 if axis == position else 1 for axis in range(len(extent))])
    return gain


def scatter_about(stream_key, extent, spread, reach, cuts=(), kind=jnp.bfloat16):
    loudness = level_of(stream_key, extent, cuts, -0.22, 0.18) if cuts else 1.0
    entries = jax.random.normal(stream_key, extent, jnp.float32) * spread * loudness
    return jnp.minimum(jnp.maximum(entries, -reach), reach).astype(kind)


def setup_inputs(seed: int = 0) -> dict:
    arg_keys = jax.random.split(jax.random.key(seed), 7)
    return {
        "records": scatter_about(arg_keys[0], (TOKENS, 3, CH), 1.0, 6.0, ((0, 512),)),
        "rec_slot": draw_rec_slot(jax.random.fold_in(arg_keys[6], 71), 0),
        "short_w": scatter_about(arg_keys[2], (3, CH, 3), 0.6, 3.0, ((1, 32),), jnp.float32),
        "residue": scatter_about(arg_keys[3], (CH, MODES), 1.0, 5.0, ((0, 32),), jnp.float32),
        "rate": jnp.clip(jnp.exp(math.log(0.03) - 6.1975026 * jax.random.uniform(arg_keys[4], (CH, MODES), jnp.float32) ** level_of(arg_keys[4], (CH, MODES), ((0, 32),), -0.2, 0.2)), 6.103515625e-05, 0.03),
        "passthrough": scatter_about(arg_keys[5], (CH,), 0.7, 4.0, ((0, 32),), jnp.float32),
    }


def reference(records, rec_slot, short_w, residue, rate, passthrough):
    record_rows = records.reshape(N_CTX * RECS, BLOCK, 3, CH)
    numbers = jnp.arange(N_CTX * RECS, dtype=jnp.int32)
    target = numbers % RECS % N_CTX * RECS + rec_slot.reshape(N_CTX * RECS).astype(jnp.int32)
    placed = jnp.zeros_like(record_rows).at[target].set(record_rows).reshape(TOKENS, 3, CH)
    stream_vals = placed.astype(jnp.float32)
    padded = jnp.concatenate([jnp.zeros((2, 3, CH), jnp.float32), stream_vals], 0)
    features = short_w[:, :, 0] * padded[2:] + short_w[:, :, 1] * padded[1:-1] + short_w[:, :, 2] * padded[:-2]
    query_gate = features[:, 0, :]
    product = features[:, 1, :] * features[:, 2, :]
    chan_block = 256 if CH % 256 == 0 else CH
    blocks = CH // chan_block
    positions = jnp.arange(TOKENS, dtype=jnp.float32)

    def one_block(operands):
        z_block, rate_block, resid_block = operands
        weights = resid_block * jnp.sqrt(2.0 * rate_block / MODES)

        def add_mode(mode_idx, impulse):
            rate_col = lax.dynamic_index_in_dim(rate_block, mode_idx, 1, keepdims=False)
            weight_col = lax.dynamic_index_in_dim(weights, mode_idx, 1, keepdims=False)
            return impulse + weight_col[None, :] * jnp.exp(-positions[:, None] * rate_col[None, :])
        impulse = lax.fori_loop(0, MODES, add_mode, jnp.zeros((TOKENS, chan_block), jnp.float32))
        spectrum = jnp.fft.rfft(z_block, n=2 * TOKENS, axis=0) * jnp.fft.rfft(impulse, n=2 * TOKENS, axis=0)
        return jnp.fft.irfft(spectrum, n=2 * TOKENS, axis=0)[:TOKENS]
    z_blocks = product.reshape(TOKENS, blocks, chan_block).transpose(1, 0, 2)
    convolved = lax.map(one_block, (z_blocks, rate.reshape(blocks, chan_block, MODES), residue.reshape(blocks, chan_block, MODES)))
    convolved = convolved.transpose(1, 0, 2).reshape(TOKENS, CH)
    return (query_gate * (convolved + passthrough * product)).astype(jnp.bfloat16)
```

```python
import functools
import math

import jax
import jax.numpy as jnp
from jax import lax
from jax.experimental import pallas as pl
from jax.experimental.pallas import tpu as pltpu
from jax.sharding import PartitionSpec as P

MESH = pl.DeviceIdType.MESH
LANES = 128
CHUNKS = 8
STRIDE = 13
MESSAGE = 32


def kernel(
    n_ctx,
    n_ch,
    block,
    modes,
    x_ref,
    slot_ref,
    w_ref,
    res_ref,
    rate_ref,
    pass_ref,
    out_ref,
    abuf,
    bbuf,
    perm,
    placed,
    pbuf,
    qbuf,
    ybuf,
    tail,
    local,
    met,
    send_a,
    recv_a,
    send_b,
    recv_b,
    send_c,
    recv_c,
):
    s = lax.axis_index("ctx")
    c = lax.axis_index("ch")
    recs = n_ch
    group = recs // n_ctx
    seq = recs * block
    steps = seq // CHUNKS
    f32 = jnp.float32

    barrier = pltpu.get_barrier_semaphore()

    @pl.loop(1, n_ch)
    def _(k):
        pl.semaphore_signal(
            barrier, inc=1, device_id={"ch": lax.rem(c + k, n_ch)}, device_id_type=MESH
        )

    @pl.loop(1, n_ctx)
    def _(k):
        pl.semaphore_signal(
            barrier, inc=1, device_id={"ctx": lax.rem(s + k, n_ctx)}, device_id_type=MESH
        )

    pl.semaphore_wait(barrier, n_ch + n_ctx - 2)

    def block_of(ch):
        return x_ref.at[:, :, pl.ds(pl.multiple_of(ch * LANES, LANES), LANES)]

    def copy_a(ch):
        return pltpu.make_async_remote_copy(
            src_ref=block_of(ch),
            dst_ref=abuf.at[c],
            send_sem=send_a.at[ch],
            recv_sem=recv_a.at[c],
            device_id={"ch": ch},
            device_id_type=MESH,
        )

    def offset(k):
        return lax.rem(STRIDE * (k + s), n_ch)

    @pl.loop(0, n_ch)
    def _(k):
        ch = lax.rem(c + offset(k), n_ch)

        @pl.when(ch != c)
        def _():
            copy_a(ch).start()

        @pl.when(ch == c)
        def _():
            pltpu.make_async_copy(block_of(c), abuf.at[c], recv_a.at[c]).start()

    col = lax.broadcasted_iota(jnp.int32, (recs, seq), 1)
    row = lax.broadcasted_iota(jnp.int32, (recs, seq), 0)
    pick = (row == (col // block) % group * n_ctx + s).astype(f32)
    spread = jnp.dot(slot_ref[...].astype(f32), pick, preferred_element_type=f32)
    col = lax.broadcasted_iota(jnp.int32, (n_ctx, seq), 1)
    row = lax.broadcasted_iota(jnp.int32, (n_ctx, seq), 0)
    spread = jnp.where(row == col // (block * group), spread, 0.0)
    target = jnp.sum(spread, axis=0, keepdims=True).astype(jnp.int32)
    target = target * block + lax.broadcasted_iota(jnp.int32, (1, seq), 1) % block
    target = target % steps * CHUNKS + target // steps

    rows_at_once = 16

    @pl.loop(0, seq // rows_at_once)
    def _(i):
        at = pl.multiple_of(i * rows_at_once, rows_at_once)
        here = lax.broadcasted_iota(jnp.int32, (rows_at_once, seq), 0) + at
        perm[pl.ds(at, rows_at_once), :] = jnp.where(here == target, 1.0, 0.0).astype(jnp.bfloat16)

    @pl.loop(s + 2, n_ctx + 1)
    def _(i):
        met[pl.ds(pl.multiple_of(i * MESSAGE, MESSAGE), MESSAGE), :] = jnp.zeros((MESSAGE, LANES), f32)

    met[0:MESSAGE, :] = jnp.zeros((MESSAGE, LANES), f32)

    def landing(source, half):
        return bbuf.at[source * group + half]

    def copy_b(r):
        return pltpu.make_async_remote_copy(
            src_ref=abuf.at[r],
            dst_ref=landing(s, r // n_ctx),
            send_sem=send_b.at[r],
            recv_sem=recv_b.at[s * group + r // n_ctx],
            device_id={"ctx": lax.rem(r, n_ctx)},
            device_id_type=MESH,
        )

    @pl.loop(0, n_ch)
    def _(k):
        r = lax.rem(c + n_ch - offset(k), n_ch)
        pltpu.make_async_copy(abuf.at[r], abuf.at[r], recv_a.at[r]).wait()
        owner = lax.rem(r, n_ctx)

        @pl.when(owner != s)
        def _():
            copy_b(r).start()

        @pl.when(owner == s)
        def _():
            i = s * group + r // n_ctx
            pltpu.make_async_copy(abuf.at[r], bbuf.at[i], recv_b.at[i]).start()

    rate = rate_ref[...]
    decay = jnp.exp(-rate)
    gain = res_ref[...] * jnp.sqrt(2.0 * rate / modes)
    chunk_id = lax.broadcasted_iota(jnp.int32, (CHUNKS, LANES), 0)

    def spread_row(table, m):
        return jnp.broadcast_to(table[m : m + 1, :], (CHUNKS, LANES))

    @pl.loop(0, n_ch)
    def _(i):
        pltpu.make_async_copy(bbuf.at[i], bbuf.at[i], recv_b.at[i]).wait()

    for j in range(3):
        placed[j] = jnp.dot(
            perm[...], bbuf[:, j].reshape(seq, LANES), preferred_element_type=f32
        )

    taps = [[jnp.broadcast_to(w_ref[j, i : i + 1, :], (CHUNKS, LANES)) for i in range(3)] for j in range(3)]
    decays = [spread_row(decay, m) for m in range(modes)]
    before = [
        [
            jnp.where(chunk_id == 0, 0.0, pltpu.roll(placed[j, (steps - i) * CHUNKS : (steps - i + 1) * CHUNKS, :], 1, 0))
            for j in range(3)
        ]
        for i in (1, 2)
    ]

    def first_pass(t, carry):
        one, two, state = carry
        at = pl.ds(pl.multiple_of(t * CHUNKS, CHUNKS), CHUNKS)
        now = [placed[j, at, :] for j in range(3)]
        feats = [taps[j][0] * now[j] + taps[j][1] * one[j] + taps[j][2] * two[j] for j in range(3)]
        product = feats[1] * feats[2]
        if isinstance(t, int):
            product = jnp.where(chunk_id == 0, 0.0, product)
        qbuf[at, :] = feats[0]
        pbuf[at, :] = product
        state = [decays[m] * state[m] + product for m in range(modes)]
        return now, one, state

    carry = (before[0], before[1], [jnp.zeros((CHUNKS, LANES), f32)] * modes)
    carry = first_pass(0, carry)
    carry = first_pass(1, carry)
    _, _, state = lax.fori_loop(2, steps, first_pass, carry, unroll=2)

    start = []
    for m in range(modes):
        total = state[m]
        for hop in (1, 2, 4):
            power = spread_row(jnp.exp(-rate[m : m + 1, :] * (steps * hop)), 0)
            total = total + power * jnp.where(chunk_id >= hop, pltpu.roll(total, hop, 0), 0.0)
        local[m : m + 1, :] = total[CHUNKS - 1 :, :]
        start.append(jnp.where(chunk_id >= 1, pltpu.roll(total, 1, 0), 0.0))
    for j in range(3):
        for i in range(2):
            local[modes + 2 * j + i : modes + 2 * j + i + 1, :] = placed[j, i * CHUNKS : i * CHUNKS + 1, :]
            at = (steps - 2 + i) * CHUNKS + CHUNKS - 1
            local[modes + 6 + 2 * j + i : modes + 7 + 2 * j + i, :] = placed[j, at : at + 1, :]
    local[modes + 12 :, :] = jnp.zeros((MESSAGE - modes - 12, LANES), f32)

    def slab(shard):
        return met.at[pl.ds(pl.multiple_of((shard + 1) * MESSAGE, MESSAGE), MESSAGE)]

    def copy_c(shard):
        return pltpu.make_async_remote_copy(
            src_ref=local,
            dst_ref=slab(s),
            send_sem=send_c.at[shard],
            recv_sem=recv_c.at[s],
            device_id={"ctx": shard},
            device_id_type=MESH,
        )

    @pl.loop(s + 1, n_ctx)
    def _(shard):
        copy_c(shard).start()

    met[pl.ds(pl.multiple_of((s + 1) * MESSAGE, MESSAGE), MESSAGE), :] = local[...]

    gains = [spread_row(gain, m) for m in range(modes)]

    def second_pass(t, state):
        at = pl.ds(pl.multiple_of(t * CHUNKS, CHUNKS), CHUNKS)
        product = pbuf[at, :]
        state = [decays[m] * state[m] + product for m in range(modes)]
        terms = [gains[m] * state[m] for m in range(modes)]
        while len(terms) > 1:
            terms = [a + b for a, b in zip(terms[::2], terms[1::2])]
        ybuf[at, :] = terms[0]
        return state

    lax.fori_loop(0, steps, second_pass, start, unroll=2)

    @pl.loop(0, s)
    def _(shard):
        pltpu.make_async_copy(slab(shard), slab(shard), recv_c.at[shard]).wait()

    def rim(row, width, base, stride):
        return met[pl.ds(base + row, width, stride=stride), :]

    def rim_products(pick_row):
        first, second = [], []
        for j in range(3):
            x0, x1 = pick_row(MESSAGE + modes + 2 * j), pick_row(MESSAGE + modes + 2 * j + 1)
            l0, l1 = pick_row(modes + 6 + 2 * j), pick_row(modes + 7 + 2 * j)
            tap = [w_ref[j, i : i + 1, :] for i in range(3)]
            first.append(tap[0] * x0 + tap[1] * l1 + tap[2] * l0)
            second.append(tap[0] * x1 + tap[1] * x0 + tap[2] * l1)
        return first[0], first[1] * first[2], second[0], second[1] * second[2]

    _, all0, _, all1 = rim_products(lambda i: met[pl.ds(i, n_ctx, stride=MESSAGE), :])
    here = met[pl.ds(pl.multiple_of(s * MESSAGE, MESSAGE), 2 * MESSAGE), :]
    q0, p0, q1, p1 = rim_products(lambda i: here[i : i + 1, :])

    back0 = jnp.exp(-rate * (seq - 1))
    back1 = jnp.exp(-rate * (seq - 2))
    entering = jnp.zeros((modes, LANES), f32)
    for shard in range(n_ctx - 1):
        behind = s - 1 - shard
        reach = jnp.exp(-rate * (seq * jnp.maximum(behind, 0)).astype(f32))
        reach = jnp.where(behind >= 0, reach, 0.0)
        ended = met[(shard + 1) * MESSAGE : (shard + 1) * MESSAGE + modes, :]
        ended = ended + back0 * all0[shard : shard + 1, :] + back1 * all1[shard : shard + 1, :]
        entering = entering + reach * ended
    grow = jnp.exp(rate)
    entering = entering + grow * (p0 + grow * p1)
    early = jnp.sum(gain * grow, axis=0, keepdims=True) * p1

    pbuf[0:1, :] = p0
    qbuf[0:1, :] = q0
    pbuf[CHUNKS : CHUNKS + 1, :] = p1
    qbuf[CHUNKS : CHUNKS + 1, :] = q1
    ybuf[0:1, :] = ybuf[0:1, :] - early

    since = (chunk_id * steps + 1).astype(f32)
    coming = [
        spread_row(gain * entering, m) * jnp.exp(-spread_row(rate, m) * since) for m in range(modes)
    ]
    direct = jnp.broadcast_to(pass_ref[...], (CHUNKS, LANES))

    def third_pass(t, coming):
        at = pl.ds(pl.multiple_of(t * CHUNKS, CHUNKS), CHUNKS)
        terms = coming
        while len(terms) > 1:
            terms = [a + b for a, b in zip(terms[::2], terms[1::2])]
        value = qbuf[at, :] * (ybuf[at, :] + terms[0] + direct * pbuf[at, :])
        tail[pl.ds(t, CHUNKS, stride=steps), :] = value
        return [decays[m] * coming[m] for m in range(modes)]

    lax.fori_loop(0, steps, third_pass, coming, unroll=2)
    out_ref[...] = tail[...].astype(out_ref.dtype)

    @pl.loop(1, n_ch)
    def _(k):
        copy_a(lax.rem(c + k, n_ch)).wait_send()

    @pl.loop(0, n_ch)
    def _(r):
        @pl.when(lax.rem(r, n_ctx) != s)
        def _():
            copy_b(r).wait_send()

    @pl.loop(s + 1, n_ctx)
    def _(shard):
        copy_c(shard).wait_send()


def shards(n_ctx, n_ch, records, rec_slot, short_w, residue, rate, passthrough):
    block, _, channels = records.shape
    modes = rate.shape[1]
    seq = n_ch * block
    f32 = jnp.float32
    vmem = pl.BlockSpec(memory_space=pltpu.VMEM)
    dma = pltpu.SemaphoreType.DMA
    return pl.pallas_call(
        functools.partial(kernel, n_ctx, n_ch, block, modes),
        out_shape=jax.ShapeDtypeStruct((seq, LANES), jnp.bfloat16),
        in_specs=[pl.BlockSpec(memory_space=pl.ANY)] + [vmem] * 5,
        out_specs=vmem,
        scratch_shapes=[
            pltpu.VMEM((n_ch, 3, block, LANES), jnp.bfloat16),
            pltpu.VMEM((n_ch, 3, block, LANES), jnp.bfloat16),
            pltpu.VMEM((seq, seq), jnp.bfloat16),
            pltpu.VMEM((3, seq, LANES), f32),
            pltpu.VMEM((seq, LANES), f32),
            pltpu.VMEM((seq, LANES), f32),
            pltpu.VMEM((seq, LANES), f32),
            pltpu.VMEM((seq, LANES), f32),
            pltpu.VMEM((MESSAGE, LANES), f32),
            pltpu.VMEM(((n_ctx + 1) * MESSAGE, LANES), f32),
            dma((n_ch,)),
            dma((n_ch,)),
            dma((n_ch,)),
            dma((n_ch,)),
            dma((n_ctx,)),
            dma((n_ctx,)),
        ],
        compiler_params=pltpu.CompilerParams(
            collective_id=0, has_side_effects=True, vmem_limit_bytes=48 * 1024 * 1024
        ),
        name="hyena",
    )(
        records.transpose(1, 0, 2),
        rec_slot,
        short_w.transpose(0, 2, 1),
        residue.T,
        rate.T,
        passthrough[None, :],
    )


def solution(mesh):
    return jax.shard_map(
        functools.partial(shards, mesh.shape["ctx"], mesh.shape["ch"]),
        mesh=mesh,
        in_specs=(
            P(("ctx", "ch"), None, None),
            P(),
            P(None, "ch", None),
            P("ch", None),
            P("ch", None),
            P("ch"),
        ),
        out_specs=P("ctx", "ch"),
        check_vma=False,
    )
```

```python
import functools

import jax
import jax.numpy as jnp
from jax import lax
from jax.experimental import pallas as pl
from jax.experimental.pallas import tpu as pltpu
from jax.sharding import PartitionSpec as P

MESH = pl.DeviceIdType.MESH
LANES = 128
CHUNKS = 8
INNER = 4
CORES = 2
MESSAGE = 32


def near_first(count):
    return [(i + 1) // 2 if i % 2 else -(i // 2) for i in range(count)]


def kernel(
    n_ctx,
    n_ch,
    block,
    modes,
    x_hbm,
    slot_hbm,
    w_hbm,
    res_hbm,
    rate_hbm,
    pass_hbm,
    out_ref,
    slot_ref,
    w_ref,
    res_ref,
    rate_ref,
    pass_ref,
    abuf,
    bbuf,
    perm,
    placed,
    pbuf,
    qbuf,
    ybuf,
    tail,
    local,
    met,
    tables,
    starts,
    load,
    send_a,
    recv_a,
    send_b,
    recv_b,
    send_c,
    recv_c,
    ready_a,
    ready_b,
):
    s = lax.axis_index("ctx")
    c = lax.axis_index("ch")
    recs = n_ch
    group = recs // n_ctx
    seq = recs * block
    steps = seq // CHUNKS
    f32 = jnp.float32
    n_z, n_y = n_ch // INNER, n_ctx // CORES

    def place_of(ctx):
        y = ctx // CORES
        return jnp.where(y == 0, 0, jnp.where(y <= n_y // 2, 2 * y - 1, 2 * (n_y - y))) * CORES + ctx % CORES

    def ctx_at(place):
        i = place // CORES
        return jnp.where(i == 0, 0, jnp.where(i % 2 == 1, (i + 1) // 2, n_y - i // 2)) * CORES + place % CORES

    place = place_of(s)

    operands = [(slot_hbm, slot_ref), (w_hbm, w_ref), (res_hbm, res_ref), (rate_hbm, rate_ref), (pass_hbm, pass_ref)]
    fetches = [pltpu.make_async_copy(src, dst, load.at[i]) for i, (src, dst) in enumerate(operands)]

    barrier = pltpu.get_barrier_semaphore()

    @pl.loop(c + 1, n_ch)
    def _(ch):
        pl.semaphore_signal(barrier, inc=1, device_id={"ch": ch}, device_id_type=MESH)

    @pl.loop(place + 1, n_ctx)
    def _(p):
        pl.semaphore_signal(barrier, inc=1, device_id={"ctx": ctx_at(p)}, device_id_type=MESH)

    def block_of(ch):
        return x_hbm.at[:, :, pl.ds(pl.multiple_of(ch * LANES, LANES), LANES)]

    pltpu.make_async_copy(block_of(c), abuf.at[c], recv_a.at[c]).start()
    for fetch in fetches:
        fetch.start()

    @pl.when(c + place > 0)
    def _():
        pl.semaphore_wait(barrier, c + place)

    def copy_a(ch):
        return pltpu.make_async_remote_copy(
            src_ref=block_of(ch),
            dst_ref=abuf.at[c],
            send_sem=send_a,
            recv_sem=recv_a.at[c],
            device_id={"ch": ch},
            device_id_type=MESH,
        )

    z, x = c // INNER, c % INNER
    offsets = [(dz, dx) for dz in near_first(n_z) for dx in range(INNER)][1:]
    for dz, dx in offsets:
        ch = (z + dz + n_z) % n_z * INNER + (x + dx) % INNER

        @pl.when(ch < c)
        def _():
            copy_a(ch).start()

    @pl.loop(0, c)
    def _(ch):
        pl.semaphore_signal(ready_a.at[c], inc=1, device_id={"ch": ch}, device_id_type=MESH)

    @pl.loop(0, place)
    def _(p):
        pl.semaphore_signal(ready_b.at[s], inc=1, device_id={"ctx": ctx_at(p)}, device_id_type=MESH)

    for fetch in fetches:
        fetch.wait()
    col = lax.broadcasted_iota(jnp.int32, (recs, seq), 1)
    row = lax.broadcasted_iota(jnp.int32, (recs, seq), 0)
    pick = (row == (col // block) % group * n_ctx + s).astype(f32)
    spread = jnp.dot(slot_ref[...].astype(f32), pick, preferred_element_type=f32)
    col = lax.broadcasted_iota(jnp.int32, (n_ctx, seq), 1)
    row = lax.broadcasted_iota(jnp.int32, (n_ctx, seq), 0)
    spread = jnp.where(row == col // (block * group), spread, 0.0)
    target = jnp.sum(spread, axis=0, keepdims=True).astype(jnp.int32)
    target = target * block + lax.broadcasted_iota(jnp.int32, (1, seq), 1) % block
    target = target % steps * CHUNKS + target // steps

    rows_at_once = 16

    @pl.loop(0, seq // rows_at_once)
    def _(i):
        at = pl.multiple_of(i * rows_at_once, rows_at_once)
        here = lax.broadcasted_iota(jnp.int32, (rows_at_once, seq), 0) + at
        perm[pl.ds(at, rows_at_once), :] = jnp.where(here == target, 1.0, 0.0).astype(jnp.bfloat16)

    @pl.loop(s + 2, n_ctx + 1)
    def _(i):
        met[pl.ds(pl.multiple_of(i * MESSAGE, MESSAGE), MESSAGE), :] = jnp.zeros((MESSAGE, LANES), f32)

    met[0:MESSAGE, :] = jnp.zeros((MESSAGE, LANES), f32)

    chunk_id = lax.broadcasted_iota(jnp.int32, (CHUNKS, LANES), 0)

    def spread_row(table, m):
        return jnp.broadcast_to(table[m : m + 1, :], (CHUNKS, LANES))

    rate = rate_ref[...]
    gain = res_ref[...] * jnp.sqrt(2.0 * rate / modes)
    grow = jnp.exp(rate)
    hops = (1, 2, 4)
    named = [jnp.exp(-rate), gain, grow, gain * grow, jnp.exp(-rate * (seq - 1)), jnp.exp(-rate * (seq - 2))]
    named += [jnp.exp(-rate * (steps * hop)) for hop in hops]
    for shard in range(n_ctx - 1):
        behind = s - 1 - shard
        reach = jnp.exp(-rate * (seq * jnp.maximum(behind, 0)).astype(f32))
        named.append(jnp.where(behind >= 0, reach, 0.0))
    for i, table in enumerate(named):
        tables[i] = table
    since = (chunk_id * steps + 1).astype(f32)
    for m in range(modes):
        starts[m] = spread_row(gain, m) * jnp.exp(-spread_row(rate, m) * since)

    @pl.loop(c + 1, n_ch)
    def _(ch):
        pl.semaphore_wait(ready_a.at[ch], 1)
        copy_a(ch).start()

    @pl.loop(place + 1, n_ctx)
    def _(p):
        pl.semaphore_wait(ready_b.at[ctx_at(p)], 1)

    def forward(r):
        pltpu.make_async_copy(abuf.at[r], abuf.at[r], recv_a.at[r]).wait()
        owner, here = r % n_ctx, s * group + r // n_ctx

        @pl.when(owner != s)
        def _():
            pltpu.make_async_remote_copy(
                src_ref=abuf.at[r],
                dst_ref=bbuf.at[here],
                send_sem=send_b,
                recv_sem=recv_b,
                device_id={"ctx": owner},
                device_id_type=MESH,
            ).start()

        @pl.when(owner == s)
        def _():
            pltpu.make_async_copy(abuf.at[r], bbuf.at[here], recv_b).start()

    for dz, dx in offsets:
        r = (z - dz + n_z) % n_z * INNER + (x - dx + INNER) % INNER

        @pl.when(r < c)
        def _():
            forward(r)

    @pl.loop(c, n_ch)
    def _(r):
        forward(r)

    pltpu.make_async_copy(bbuf, bbuf, recv_b).wait()

    def table(i):
        return tables[i]

    def table_row(i, m):
        return jnp.broadcast_to(tables[i, m : m + 1, :], (CHUNKS, LANES))

    for j in range(3):
        placed[j] = jnp.dot(
            perm[...], bbuf[:, j].reshape(seq, LANES), preferred_element_type=f32
        )

    taps = [[jnp.broadcast_to(w_ref[j, i : i + 1, :], (CHUNKS, LANES)) for i in range(3)] for j in range(3)]
    decays = [table_row(0, m) for m in range(modes)]
    before = [
        [
            jnp.where(chunk_id == 0, 0.0, pltpu.roll(placed[j, (steps - i) * CHUNKS : (steps - i + 1) * CHUNKS, :], 1, 0))
            for j in range(3)
        ]
        for i in (1, 2)
    ]

    def first_pass(t, carry):
        one, two, state = carry
        at = pl.ds(pl.multiple_of(t * CHUNKS, CHUNKS), CHUNKS)
        now = [placed[j, at, :] for j in range(3)]
        feats = [taps[j][0] * now[j] + taps[j][1] * one[j] + taps[j][2] * two[j] for j in range(3)]
        product = feats[1] * feats[2]
        if isinstance(t, int):
            product = jnp.where(chunk_id == 0, 0.0, product)
        qbuf[at, :] = feats[0]
        pbuf[at, :] = product
        state = [decays[m] * state[m] + product for m in range(modes)]
        return now, one, state

    carry = (before[0], before[1], [jnp.zeros((CHUNKS, LANES), f32)] * modes)
    carry = first_pass(0, carry)
    carry = first_pass(1, carry)
    _, _, state = lax.fori_loop(2, steps, first_pass, carry, unroll=2)

    start = []
    for m in range(modes):
        total = state[m]
        for i, hop in enumerate(hops):
            total = total + table_row(6 + i, m) * jnp.where(chunk_id >= hop, pltpu.roll(total, hop, 0), 0.0)
        local[m : m + 1, :] = total[CHUNKS - 1 :, :]
        start.append(jnp.where(chunk_id >= 1, pltpu.roll(total, 1, 0), 0.0))
    for j in range(3):
        for i in range(2):
            local[modes + 2 * j + i : modes + 2 * j + i + 1, :] = placed[j, i * CHUNKS : i * CHUNKS + 1, :]
            at = (steps - 2 + i) * CHUNKS + CHUNKS - 1
            local[modes + 6 + 2 * j + i : modes + 7 + 2 * j + i, :] = placed[j, at : at + 1, :]
    local[modes + 12 :, :] = jnp.zeros((MESSAGE - modes - 12, LANES), f32)

    def slab(shard):
        return met.at[pl.ds(pl.multiple_of((shard + 1) * MESSAGE, MESSAGE), MESSAGE)]

    def copy_c(shard):
        return pltpu.make_async_remote_copy(
            src_ref=local,
            dst_ref=slab(s),
            send_sem=send_c.at[shard],
            recv_sem=recv_c.at[s],
            device_id={"ctx": shard},
            device_id_type=MESH,
        )

    @pl.loop(s + 1, n_ctx)
    def _(shard):
        copy_c(shard).start()

    met[pl.ds(pl.multiple_of((s + 1) * MESSAGE, MESSAGE), MESSAGE), :] = local[...]

    gains = [table_row(1, m) for m in range(modes)]

    def second_pass(t, state):
        at = pl.ds(pl.multiple_of(t * CHUNKS, CHUNKS), CHUNKS)
        product = pbuf[at, :]
        state = [decays[m] * state[m] + product for m in range(modes)]
        terms = [gains[m] * state[m] for m in range(modes)]
        while len(terms) > 1:
            terms = [a + b for a, b in zip(terms[::2], terms[1::2])]
        ybuf[at, :] = terms[0]
        return state

    lax.fori_loop(0, steps, second_pass, start, unroll=2)

    @pl.loop(0, s)
    def _(shard):
        pltpu.make_async_copy(slab(shard), slab(shard), recv_c.at[shard]).wait()

    def rim(row, width, base, stride):
        return met[pl.ds(base + row, width, stride=stride), :]

    def rim_products(pick_row):
        first, second = [], []
        for j in range(3):
            x0, x1 = pick_row(MESSAGE + modes + 2 * j), pick_row(MESSAGE + modes + 2 * j + 1)
            l0, l1 = pick_row(modes + 6 + 2 * j), pick_row(modes + 7 + 2 * j)
            tap = [w_ref[j, i : i + 1, :] for i in range(3)]
            first.append(tap[0] * x0 + tap[1] * l1 + tap[2] * l0)
            second.append(tap[0] * x1 + tap[1] * x0 + tap[2] * l1)
        return first[0], first[1] * first[2], second[0], second[1] * second[2]

    _, all0, _, all1 = rim_products(lambda i: met[pl.ds(i, n_ctx, stride=MESSAGE), :])
    here = met[pl.ds(pl.multiple_of(s * MESSAGE, MESSAGE), 2 * MESSAGE), :]
    q0, p0, q1, p1 = rim_products(lambda i: here[i : i + 1, :])

    entering = jnp.zeros((modes, LANES), f32)
    for shard in range(n_ctx - 1):
        ended = met[(shard + 1) * MESSAGE : (shard + 1) * MESSAGE + modes, :]
        ended = ended + table(4) * all0[shard : shard + 1, :] + table(5) * all1[shard : shard + 1, :]
        entering = entering + table(9 + shard) * ended
    entering = entering + table(2) * (p0 + table(2) * p1)
    early = jnp.sum(table(3), axis=0, keepdims=True) * p1

    pbuf[0:1, :] = p0
    qbuf[0:1, :] = q0
    pbuf[CHUNKS : CHUNKS + 1, :] = p1
    qbuf[CHUNKS : CHUNKS + 1, :] = q1
    ybuf[0:1, :] = ybuf[0:1, :] - early

    coming = [starts[m] * spread_row(entering, m) for m in range(modes)]
    direct = jnp.broadcast_to(pass_ref[...], (CHUNKS, LANES))

    def third_pass(t, coming):
        at = pl.ds(pl.multiple_of(t * CHUNKS, CHUNKS), CHUNKS)
        terms = coming
        while len(terms) > 1:
            terms = [a + b for a, b in zip(terms[::2], terms[1::2])]
        value = qbuf[at, :] * (ybuf[at, :] + terms[0] + direct * pbuf[at, :])
        tail[pl.ds(t, CHUNKS, stride=steps), :] = value
        return [decays[m] * coming[m] for m in range(modes)]

    lax.fori_loop(0, steps, third_pass, coming, unroll=2)
    out_ref[...] = tail[...].astype(out_ref.dtype)

    pltpu.make_async_copy(abuf.at[1:], abuf.at[1:], send_a).wait()
    pltpu.make_async_copy(abuf.at[group:], abuf.at[group:], send_b).wait()

    @pl.loop(s + 1, n_ctx)
    def _(shard):
        copy_c(shard).wait_send()


def shards(n_ctx, n_ch, records, rec_slot, short_w, residue, rate, passthrough):
    block, _, channels = records.shape
    modes = rate.shape[1]
    seq = n_ch * block
    f32 = jnp.float32
    vmem = pl.BlockSpec(memory_space=pltpu.VMEM)
    dma = pltpu.SemaphoreType.DMA
    return pl.pallas_call(
        functools.partial(kernel, n_ctx, n_ch, block, modes),
        out_shape=jax.ShapeDtypeStruct((seq, LANES), jnp.bfloat16),
        in_specs=[pl.BlockSpec(memory_space=pl.ANY)] * 6,
        out_specs=vmem,
        scratch_shapes=[
            pltpu.VMEM(rec_slot.shape, jnp.int32),
            pltpu.VMEM((3, 3, LANES), f32),
            pltpu.VMEM((modes, LANES), f32),
            pltpu.VMEM((modes, LANES), f32),
            pltpu.VMEM((1, LANES), f32),
            pltpu.VMEM((n_ch, 3, block, LANES), jnp.bfloat16),
            pltpu.VMEM((n_ch, 3, block, LANES), jnp.bfloat16),
            pltpu.VMEM((seq, seq), jnp.bfloat16),
            pltpu.VMEM((3, seq, LANES), f32),
            pltpu.VMEM((seq, LANES), f32),
            pltpu.VMEM((seq, LANES), f32),
            pltpu.VMEM((seq, LANES), f32),
            pltpu.VMEM((seq, LANES), f32),
            pltpu.VMEM((MESSAGE, LANES), f32),
            pltpu.VMEM(((n_ctx + 1) * MESSAGE, LANES), f32),
            pltpu.VMEM((8 + n_ctx, modes, LANES), f32),
            pltpu.VMEM((modes, CHUNKS, LANES), f32),
            dma((5,)),
            dma,
            dma((n_ch,)),
            dma,
            dma,
            dma((n_ctx,)),
            dma((n_ctx,)),
            pltpu.SemaphoreType.REGULAR((n_ch,)),
            pltpu.SemaphoreType.REGULAR((n_ctx,)),
        ],
        compiler_params=pltpu.CompilerParams(
            collective_id=0, has_side_effects=True, vmem_limit_bytes=61 * 1024 * 1024
        ),
        name="hyena",
    )(
        records.transpose(1, 0, 2),
        rec_slot,
        short_w.transpose(0, 2, 1),
        residue.T,
        rate.T,
        passthrough[None, :],
    )


def solution(mesh):
    return jax.shard_map(
        functools.partial(shards, mesh.shape["ctx"], mesh.shape["ch"]),
        mesh=mesh,
        in_specs=(
            P(("ctx", "ch"), None, None),
            P(),
            P(None, "ch", None),
            P("ch", None),
            P("ch", None),
            P("ch"),
        ),
        out_specs=P("ctx", "ch"),
        check_vma=False,
    )
```

```python
import functools

import jax
import jax.numpy as jnp
from jax import lax
from jax.experimental import pallas as pl
from jax.experimental.pallas import tpu as pltpu
from jax.sharding import PartitionSpec as P

MESH = pl.DeviceIdType.MESH
LANES = 128
CHUNKS = 8
INNER = 4
CORES = 2
MESSAGE = 32


def near_first(count):
    return [(i + 1) // 2 if i % 2 else -(i // 2) for i in range(count)]


def kernel(
    n_ctx,
    n_ch,
    block,
    modes,
    x_hbm,
    slot_hbm,
    w_hbm,
    res_hbm,
    rate_hbm,
    pass_hbm,
    out_ref,
    slot_ref,
    w_ref,
    res_ref,
    rate_ref,
    pass_ref,
    abuf,
    bbuf,
    perm,
    placed,
    pbuf,
    qbuf,
    ybuf,
    tail,
    local,
    sent,
    met,
    got,
    tables,
    starts,
    load,
    send_a,
    recv_a,
    send_b,
    recv_b,
    send_c,
    recv_c,
    ready_a,
    ready_b,
):
    s = lax.axis_index("ctx")
    c = lax.axis_index("ch")
    recs = n_ch
    group = recs // n_ctx
    seq = recs * block
    steps = seq // CHUNKS
    f32 = jnp.float32
    n_z, n_y = n_ch // INNER, n_ctx // CORES

    def place_of(ctx):
        y = ctx // CORES
        return jnp.where(y == 0, 0, jnp.where(y <= n_y // 2, 2 * y - 1, 2 * (n_y - y))) * CORES + ctx % CORES

    def ctx_at(place):
        i = place // CORES
        return jnp.where(i == 0, 0, jnp.where(i % 2 == 1, (i + 1) // 2, n_y - i // 2)) * CORES + place % CORES

    place = place_of(s)

    operands = [(slot_hbm, slot_ref), (w_hbm, w_ref), (res_hbm, res_ref), (rate_hbm, rate_ref), (pass_hbm, pass_ref)]
    fetches = [pltpu.make_async_copy(src, dst, load.at[i]) for i, (src, dst) in enumerate(operands)]

    barrier = pltpu.get_barrier_semaphore()

    @pl.loop(c + 1, n_ch)
    def _(ch):
        pl.semaphore_signal(barrier, inc=1, device_id={"ch": ch}, device_id_type=MESH)

    @pl.loop(place + 1, n_ctx)
    def _(p):
        pl.semaphore_signal(barrier, inc=1, device_id={"ctx": ctx_at(p)}, device_id_type=MESH)

    def block_of(ch):
        return x_hbm.at[:, :, pl.ds(pl.multiple_of(ch * LANES, LANES), LANES)]

    pltpu.make_async_copy(block_of(c), abuf.at[c], recv_a.at[c]).start()
    for fetch in fetches:
        fetch.start()

    @pl.when(c + place > 0)
    def _():
        pl.semaphore_wait(barrier, c + place)

    def copy_a(ch):
        return pltpu.make_async_remote_copy(
            src_ref=block_of(ch),
            dst_ref=abuf.at[c],
            send_sem=send_a,
            recv_sem=recv_a.at[c],
            device_id={"ch": ch},
            device_id_type=MESH,
        )

    z, x = c // INNER, c % INNER
    offsets = [(dz, dx) for dz in near_first(n_z) for dx in range(INNER)][1:]
    for dz, dx in offsets:
        ch = (z + dz + n_z) % n_z * INNER + (x + dx) % INNER

        @pl.when(ch < c)
        def _():
            copy_a(ch).start()

    @pl.loop(0, c)
    def _(ch):
        pl.semaphore_signal(ready_a.at[c], inc=1, device_id={"ch": ch}, device_id_type=MESH)

    @pl.loop(0, place)
    def _(p):
        pl.semaphore_signal(ready_b.at[s], inc=1, device_id={"ctx": ctx_at(p)}, device_id_type=MESH)

    for fetch in fetches:
        fetch.wait()
    col = lax.broadcasted_iota(jnp.int32, (recs, seq), 1)
    row = lax.broadcasted_iota(jnp.int32, (recs, seq), 0)
    pick = (row == (col // block) % group * n_ctx + s).astype(f32)
    spread = jnp.dot(slot_ref[...].astype(f32), pick, preferred_element_type=f32)
    col = lax.broadcasted_iota(jnp.int32, (n_ctx, seq), 1)
    row = lax.broadcasted_iota(jnp.int32, (n_ctx, seq), 0)
    spread = jnp.where(row == col // (block * group), spread, 0.0)
    target = jnp.sum(spread, axis=0, keepdims=True).astype(jnp.int32)
    target = target * block + lax.broadcasted_iota(jnp.int32, (1, seq), 1) % block
    target = target % steps * CHUNKS + target // steps

    rows_at_once = 16

    @pl.loop(0, seq // rows_at_once)
    def _(i):
        at = pl.multiple_of(i * rows_at_once, rows_at_once)
        here = lax.broadcasted_iota(jnp.int32, (rows_at_once, seq), 0) + at
        perm[pl.ds(at, rows_at_once), :] = jnp.where(here == target, 1.0, 0.0).astype(jnp.bfloat16)

    @pl.loop(s + 2, n_ctx + 1)
    def _(i):
        met[pl.ds(pl.multiple_of(i * MESSAGE, MESSAGE), MESSAGE), :] = jnp.zeros((MESSAGE, LANES), jnp.bfloat16)

    met[0:MESSAGE, :] = jnp.zeros((MESSAGE, LANES), jnp.bfloat16)

    chunk_id = lax.broadcasted_iota(jnp.int32, (CHUNKS, LANES), 0)

    def spread_row(table, m):
        return jnp.broadcast_to(table[m : m + 1, :], (CHUNKS, LANES))

    rate = rate_ref[...]
    gain = res_ref[...] * jnp.sqrt(2.0 * rate / modes)
    grow = jnp.exp(rate)
    hops = (1, 2, 4)
    named = [jnp.exp(-rate), gain, grow, gain * grow, jnp.exp(-rate * (seq - 1)), jnp.exp(-rate * (seq - 2))]
    named += [jnp.exp(-rate * (steps * hop)) for hop in hops]
    for shard in range(n_ctx - 1):
        behind = s - 1 - shard
        reach = jnp.exp(-rate * (seq * jnp.maximum(behind, 0)).astype(f32))
        named.append(jnp.where(behind >= 0, reach, 0.0))
    for i, table in enumerate(named):
        tables[i] = table
    since = (chunk_id * steps + 1).astype(f32)
    for m in range(modes):
        starts[m] = spread_row(gain, m) * jnp.exp(-spread_row(rate, m) * since)

    @pl.loop(c + 1, n_ch)
    def _(ch):
        pl.semaphore_wait(ready_a.at[ch], 1)
        copy_a(ch).start()

    @pl.loop(place + 1, n_ctx)
    def _(p):
        pl.semaphore_wait(ready_b.at[ctx_at(p)], 1)

    def forward(r):
        pltpu.make_async_copy(abuf.at[r], abuf.at[r], recv_a.at[r]).wait()
        owner, here = r % n_ctx, s * group + r // n_ctx

        @pl.when(owner != s)
        def _():
            pltpu.make_async_remote_copy(
                src_ref=abuf.at[r],
                dst_ref=bbuf.at[here],
                send_sem=send_b,
                recv_sem=recv_b,
                device_id={"ctx": owner},
                device_id_type=MESH,
            ).start()

        @pl.when(owner == s)
        def _():
            pltpu.make_async_copy(abuf.at[r], bbuf.at[here], recv_b).start()

    for dz, dx in offsets:
        r = (z - dz + n_z) % n_z * INNER + (x - dx + INNER) % INNER

        @pl.when(r < c)
        def _():
            forward(r)

    @pl.loop(c, n_ch)
    def _(r):
        forward(r)

    pltpu.make_async_copy(bbuf, bbuf, recv_b).wait()

    def table(i):
        return tables[i]

    def table_row(i, m):
        return jnp.broadcast_to(tables[i, m : m + 1, :], (CHUNKS, LANES))

    for j in range(3):
        placed[j] = jnp.dot(
            perm[...], bbuf[:, j].reshape(seq, LANES), preferred_element_type=f32
        )

    taps = [[jnp.broadcast_to(w_ref[j, i : i + 1, :], (CHUNKS, LANES)) for i in range(3)] for j in range(3)]
    decays = [table_row(0, m) for m in range(modes)]
    before = [
        [
            jnp.where(chunk_id == 0, 0.0, pltpu.roll(placed[j, (steps - i) * CHUNKS : (steps - i + 1) * CHUNKS, :], 1, 0))
            for j in range(3)
        ]
        for i in (1, 2)
    ]

    def first_pass(t, carry):
        one, two, state = carry
        at = pl.ds(pl.multiple_of(t * CHUNKS, CHUNKS), CHUNKS)
        now = [placed[j, at, :] for j in range(3)]
        feats = [taps[j][0] * now[j] + taps[j][1] * one[j] + taps[j][2] * two[j] for j in range(3)]
        product = feats[1] * feats[2]
        if isinstance(t, int):
            product = jnp.where(chunk_id == 0, 0.0, product)
        qbuf[at, :] = feats[0]
        pbuf[at, :] = product
        state = [decays[m] * state[m] + product for m in range(modes)]
        return now, one, state

    carry = (before[0], before[1], [jnp.zeros((CHUNKS, LANES), f32)] * modes)
    carry = first_pass(0, carry)
    carry = first_pass(1, carry)
    _, _, state = lax.fori_loop(2, steps, first_pass, carry, unroll=2)

    start = []
    for m in range(modes):
        total = state[m]
        for i, hop in enumerate(hops):
            total = total + table_row(6 + i, m) * jnp.where(chunk_id >= hop, pltpu.roll(total, hop, 0), 0.0)
        local[m : m + 1, :] = total[CHUNKS - 1 :, :]
        start.append(jnp.where(chunk_id >= 1, pltpu.roll(total, 1, 0), 0.0))
    for j in range(3):
        for i in range(2):
            local[modes + 2 * j + i : modes + 2 * j + i + 1, :] = placed[j, i * CHUNKS : i * CHUNKS + 1, :]
            at = (steps - 2 + i) * CHUNKS + CHUNKS - 1
            local[modes + 6 + 2 * j + i : modes + 7 + 2 * j + i, :] = placed[j, at : at + 1, :]
    local[modes + 12 :, :] = jnp.zeros((MESSAGE - modes - 12, LANES), f32)
    sent[...] = local[...].astype(jnp.bfloat16)

    def slab(shard):
        return met.at[pl.ds(pl.multiple_of((shard + 1) * MESSAGE, MESSAGE), MESSAGE)]

    def copy_c(shard):
        return pltpu.make_async_remote_copy(
            src_ref=sent,
            dst_ref=slab(s),
            send_sem=send_c.at[shard],
            recv_sem=recv_c.at[s],
            device_id={"ctx": shard},
            device_id_type=MESH,
        )

    @pl.loop(s + 1, n_ctx)
    def _(shard):
        copy_c(shard).start()

    met[pl.ds(pl.multiple_of((s + 1) * MESSAGE, MESSAGE), MESSAGE), :] = sent[...]

    gains = [table_row(1, m) for m in range(modes)]

    def second_pass(t, state):
        at = pl.ds(pl.multiple_of(t * CHUNKS, CHUNKS), CHUNKS)
        product = pbuf[at, :]
        state = [decays[m] * state[m] + product for m in range(modes)]
        terms = [gains[m] * state[m] for m in range(modes)]
        while len(terms) > 1:
            terms = [a + b for a, b in zip(terms[::2], terms[1::2])]
        ybuf[at, :] = terms[0]
        return state

    lax.fori_loop(0, steps, second_pass, start, unroll=2)

    @pl.loop(0, s)
    def _(shard):
        pltpu.make_async_copy(slab(shard), slab(shard), recv_c.at[shard]).wait()

    got[...] = met[...].astype(f32)

    def rim_products(pick_row):
        first, second = [], []
        for j in range(3):
            x0, x1 = pick_row(MESSAGE + modes + 2 * j), pick_row(MESSAGE + modes + 2 * j + 1)
            l0, l1 = pick_row(modes + 6 + 2 * j), pick_row(modes + 7 + 2 * j)
            tap = [w_ref[j, i : i + 1, :] for i in range(3)]
            first.append(tap[0] * x0 + tap[1] * l1 + tap[2] * l0)
            second.append(tap[0] * x1 + tap[1] * x0 + tap[2] * l1)
        return first[0], first[1] * first[2], second[0], second[1] * second[2]

    _, all0, _, all1 = rim_products(lambda i: got[pl.ds(i, n_ctx, stride=MESSAGE), :])
    here = got[pl.ds(pl.multiple_of(s * MESSAGE, MESSAGE), 2 * MESSAGE), :]
    q0, p0, q1, p1 = rim_products(lambda i: here[i : i + 1, :])

    entering = jnp.zeros((modes, LANES), f32)
    for shard in range(n_ctx - 1):
        ended = got[(shard + 1) * MESSAGE : (shard + 1) * MESSAGE + modes, :]
        ended = ended + table(4) * all0[shard : shard + 1, :] + table(5) * all1[shard : shard + 1, :]
        entering = entering + table(9 + shard) * ended
    entering = entering + table(2) * (p0 + table(2) * p1)
    early = jnp.sum(table(3), axis=0, keepdims=True) * p1

    pbuf[0:1, :] = p0
    qbuf[0:1, :] = q0
    pbuf[CHUNKS : CHUNKS + 1, :] = p1
    qbuf[CHUNKS : CHUNKS + 1, :] = q1
    ybuf[0:1, :] = ybuf[0:1, :] - early

    coming = [starts[m] * spread_row(entering, m) for m in range(modes)]
    direct = jnp.broadcast_to(pass_ref[...], (CHUNKS, LANES))

    def third_pass(t, coming):
        at = pl.ds(pl.multiple_of(t * CHUNKS, CHUNKS), CHUNKS)
        terms = coming
        while len(terms) > 1:
            terms = [a + b for a, b in zip(terms[::2], terms[1::2])]
        value = qbuf[at, :] * (ybuf[at, :] + terms[0] + direct * pbuf[at, :])
        tail[pl.ds(t, CHUNKS, stride=steps), :] = value
        return [decays[m] * coming[m] for m in range(modes)]

    lax.fori_loop(0, steps, third_pass, coming, unroll=2)
    out_ref[...] = tail[...].astype(out_ref.dtype)

    pltpu.make_async_copy(abuf.at[1:], abuf.at[1:], send_a).wait()
    pltpu.make_async_copy(abuf.at[group:], abuf.at[group:], send_b).wait()

    @pl.loop(s + 1, n_ctx)
    def _(shard):
        copy_c(shard).wait_send()


def shards(n_ctx, n_ch, records, rec_slot, short_w, residue, rate, passthrough):
    block, _, channels = records.shape
    modes = rate.shape[1]
    seq = n_ch * block
    f32 = jnp.float32
    vmem = pl.BlockSpec(memory_space=pltpu.VMEM)
    dma = pltpu.SemaphoreType.DMA
    return pl.pallas_call(
        functools.partial(kernel, n_ctx, n_ch, block, modes),
        out_shape=pltpu.VMEM((seq, LANES), jnp.bfloat16),
        in_specs=[pl.BlockSpec(memory_space=pl.ANY)] * 6,
        out_specs=vmem,
        scratch_shapes=[
            pltpu.VMEM(rec_slot.shape, jnp.int32),
            pltpu.VMEM((3, 3, LANES), f32),
            pltpu.VMEM((modes, LANES), f32),
            pltpu.VMEM((modes, LANES), f32),
            pltpu.VMEM((1, LANES), f32),
            pltpu.VMEM((n_ch, 3, block, LANES), jnp.bfloat16),
            pltpu.VMEM((n_ch, 3, block, LANES), jnp.bfloat16),
            pltpu.VMEM((seq, seq), jnp.bfloat16),
            pltpu.VMEM((3, seq, LANES), f32),
            pltpu.VMEM((seq, LANES), f32),
            pltpu.VMEM((seq, LANES), f32),
            pltpu.VMEM((seq, LANES), f32),
            pltpu.VMEM((seq, LANES), f32),
            pltpu.VMEM((MESSAGE, LANES), f32),
            pltpu.VMEM((MESSAGE, LANES), jnp.bfloat16),
            pltpu.VMEM(((n_ctx + 1) * MESSAGE, LANES), jnp.bfloat16),
            pltpu.VMEM(((n_ctx + 1) * MESSAGE, LANES), f32),
            pltpu.VMEM((8 + n_ctx, modes, LANES), f32),
            pltpu.VMEM((modes, CHUNKS, LANES), f32),
            dma((5,)),
            dma,
            dma((n_ch,)),
            dma,
            dma,
            dma((n_ctx,)),
            dma((n_ctx,)),
            pltpu.SemaphoreType.REGULAR((n_ch,)),
            pltpu.SemaphoreType.REGULAR((n_ctx,)),
        ],
        compiler_params=pltpu.CompilerParams(
            collective_id=0, has_side_effects=True, vmem_limit_bytes=61 * 1024 * 1024
        ),
        name="hyena",
    )(
        records.transpose(1, 0, 2),
        rec_slot,
        short_w.transpose(0, 2, 1),
        residue.T,
        rate.T,
        passthrough[None, :],
    )


def solution(mesh):
    return jax.shard_map(
        functools.partial(shards, mesh.shape["ctx"], mesh.shape["ch"]),
        mesh=mesh,
        in_specs=(
            P(("ctx", "ch"), None, None),
            P(),
            P(None, "ch", None),
            P("ch", None),
            P("ch", None),
            P("ch"),
        ),
        out_specs=P("ctx", "ch"),
        check_vma=False,
    )
```

```python
import functools

import jax
import jax.numpy as jnp
from jax import lax
from jax.experimental import pallas as pl
from jax.experimental.pallas import tpu as pltpu
from jax.sharding import PartitionSpec as P

MESH = pl.DeviceIdType.MESH
LANES = 128
CHUNKS = 8
INNER = 4
CORES = 2
MESSAGE = 32


def near_first(count):
    return [(i + 1) // 2 if i % 2 else -(i // 2) for i in range(count)]


def kernel(
    n_ctx,
    n_ch,
    block,
    modes,
    x_hbm,
    slot_hbm,
    w_hbm,
    res_hbm,
    rate_hbm,
    pass_hbm,
    out_ref,
    x_ref,
    slot_ref,
    w_ref,
    res_ref,
    rate_ref,
    pass_ref,
    abuf,
    bbuf,
    perm,
    placed,
    pbuf,
    qbuf,
    ybuf,
    tail,
    local,
    sent,
    met,
    got,
    tables,
    starts,
    load,
    send_a,
    recv_a,
    send_b,
    recv_b,
    send_c,
    recv_c,
    ready_a,
    ready_b,
):
    s = lax.axis_index("ctx")
    c = lax.axis_index("ch")
    recs = n_ch
    group = recs // n_ctx
    seq = recs * block
    steps = seq // CHUNKS
    f32 = jnp.float32
    n_z, n_y = n_ch // INNER, n_ctx // CORES

    def place_of(ctx):
        y = ctx // CORES
        return jnp.where(y == 0, 0, jnp.where(y <= n_y // 2, 2 * y - 1, 2 * (n_y - y))) * CORES + ctx % CORES

    def ctx_at(place):
        i = place // CORES
        return jnp.where(i == 0, 0, jnp.where(i % 2 == 1, (i + 1) // 2, n_y - i // 2)) * CORES + place % CORES

    place = place_of(s)

    operands = [(slot_hbm, slot_ref), (w_hbm, w_ref), (res_hbm, res_ref), (rate_hbm, rate_ref), (pass_hbm, pass_ref)]
    fetches = [pltpu.make_async_copy(src, dst, load.at[i]) for i, (src, dst) in enumerate(operands)]

    barrier = pltpu.get_barrier_semaphore()

    @pl.loop(c + 1, n_ch)
    def _(ch):
        pl.semaphore_signal(barrier, inc=1, device_id={"ch": ch}, device_id_type=MESH)

    @pl.loop(place + 1, n_ctx)
    def _(p):
        pl.semaphore_signal(barrier, inc=1, device_id={"ctx": ctx_at(p)}, device_id_type=MESH)

    def block_of(ch, source=x_hbm):
        return source.at[:, :, pl.ds(pl.multiple_of(ch * LANES, LANES), LANES)]

    pltpu.make_async_copy(block_of(c), abuf.at[c], recv_a.at[c]).start()
    x_copy = pltpu.make_async_copy(x_hbm, x_ref, load.at[5])
    x_copy.start()
    for fetch in fetches:
        fetch.start()

    @pl.when(c + place > 0)
    def _():
        pl.semaphore_wait(barrier, c + place)

    def copy_a(ch, source=x_hbm):
        return pltpu.make_async_remote_copy(
            src_ref=block_of(ch, source),
            dst_ref=abuf.at[c],
            send_sem=send_a,
            recv_sem=recv_a.at[c],
            device_id={"ch": ch},
            device_id_type=MESH,
        )

    z, x = c // INNER, c % INNER
    offsets = [(dz, dx) for dz in near_first(n_z) for dx in range(INNER)][1:]
    for i in range(n_ch):
        ch = i // INNER * INNER + (x + i) % INNER

        @pl.when(ch < c)
        def _():
            pl.semaphore_signal(ready_a.at[c], inc=1, device_id={"ch": ch}, device_id_type=MESH)
            copy_a(ch).start()

    @pl.loop(0, place)
    def _(p):
        pl.semaphore_signal(ready_b.at[s], inc=1, device_id={"ctx": ctx_at(p)}, device_id_type=MESH)

    half = n_ch // 2

    def send_later(ch):
        pl.semaphore_wait(ready_a.at[ch], 1)
        copy_a(ch, x_ref).start()

    x_copy.wait()
    pl.loop(c + 1, jnp.where(c < half, half, n_ch))(send_later)

    for fetch in fetches:
        fetch.wait()
    col = lax.broadcasted_iota(jnp.int32, (recs, seq), 1)
    row = lax.broadcasted_iota(jnp.int32, (recs, seq), 0)
    pick = (row == (col // block) % group * n_ctx + s).astype(f32)
    spread = jnp.dot(slot_ref[...].astype(f32), pick, preferred_element_type=f32)
    col = lax.broadcasted_iota(jnp.int32, (n_ctx, seq), 1)
    row = lax.broadcasted_iota(jnp.int32, (n_ctx, seq), 0)
    spread = jnp.where(row == col // (block * group), spread, 0.0)
    target = jnp.sum(spread, axis=0, keepdims=True).astype(jnp.int32)
    target = target * block + lax.broadcasted_iota(jnp.int32, (1, seq), 1) % block
    target = target % steps * CHUNKS + target // steps

    rows_at_once = 16

    @pl.loop(0, seq // rows_at_once)
    def _(i):
        at = pl.multiple_of(i * rows_at_once, rows_at_once)
        here = lax.broadcasted_iota(jnp.int32, (rows_at_once, seq), 0) + at
        perm[pl.ds(at, rows_at_once), :] = jnp.where(here == target, 1.0, 0.0).astype(jnp.bfloat16)

    @pl.loop(s + 2, n_ctx + 1)
    def _(i):
        met[pl.ds(pl.multiple_of(i * MESSAGE, MESSAGE), MESSAGE), :] = jnp.zeros((MESSAGE, LANES), jnp.bfloat16)

    met[0:MESSAGE, :] = jnp.zeros((MESSAGE, LANES), jnp.bfloat16)

    chunk_id = lax.broadcasted_iota(jnp.int32, (CHUNKS, LANES), 0)

    def spread_row(table, m):
        return jnp.broadcast_to(table[m : m + 1, :], (CHUNKS, LANES))

    rate = rate_ref[...]
    gain = res_ref[...] * jnp.sqrt(2.0 * rate / modes)
    grow = jnp.exp(rate)
    hops = (1, 2, 4)
    named = [jnp.exp(-rate), gain, grow, gain * grow, jnp.exp(-rate * (seq - 1)), jnp.exp(-rate * (seq - 2))]
    named += [jnp.exp(-rate * (steps * hop)) for hop in hops]
    for shard in range(n_ctx - 1):
        behind = s - 1 - shard
        reach = jnp.exp(-rate * (seq * jnp.maximum(behind, 0)).astype(f32))
        named.append(jnp.where(behind >= 0, reach, 0.0))
    for i, table in enumerate(named):
        tables[i] = table
    since = (chunk_id * steps + 1).astype(f32)
    for m in range(modes):
        starts[m] = spread_row(gain, m) * jnp.exp(-spread_row(rate, m) * since)

    pl.loop(half, jnp.where(c < half, n_ch, half))(send_later)

    def forward(r):
        pltpu.make_async_copy(abuf.at[r], abuf.at[r], recv_a.at[r]).wait()
        owner, here = r % n_ctx, s * group + r // n_ctx

        @pl.when(owner != s)
        def _():
            pltpu.make_async_remote_copy(
                src_ref=abuf.at[r],
                dst_ref=bbuf.at[here],
                send_sem=send_b,
                recv_sem=recv_b,
                device_id={"ctx": owner},
                device_id_type=MESH,
            ).start()

        @pl.when(owner == s)
        def _():
            pltpu.make_async_copy(abuf.at[r], bbuf.at[here], recv_b).start()

    def first(r):
        @pl.when(place_of(r) > place)
        def _():
            pl.semaphore_wait(ready_b.at[r], 1)

        forward(r)

    @pl.when(c < n_ch // 2)
    def _():
        for dz, dx in offsets:
            r = (z - dz + n_z) % n_z * INNER + (x - dx + INNER) % INNER

            @pl.when((r < c) & (r < n_ctx))
            def _():
                first(r)

        @pl.loop(c, n_ctx)
        def _(r):
            first(r)

        for dz, dx in offsets:
            r = (z - dz + n_z) % n_z * INNER + (x - dx + INNER) % INNER

            @pl.when((r < c) & (r >= n_ctx))
            def _():
                forward(r)

        @pl.loop(jnp.maximum(c, n_ctx), n_ch)
        def _(r):
            forward(r)


    @pl.when(c >= n_ch // 2)
    def _():
        @pl.loop(0, n_ctx)
        def _(k):
            first((s + n_ctx - 1 - k) % n_ctx)

        @pl.loop(0, n_ctx)
        def _(k):
            forward((s + n_ctx - 1 - k) % n_ctx + n_ctx)


    pltpu.make_async_copy(bbuf, bbuf, recv_b).wait()

    def table(i):
        return tables[i]

    def table_row(i, m):
        return jnp.broadcast_to(tables[i, m : m + 1, :], (CHUNKS, LANES))

    for j in range(3):
        placed[j] = jnp.dot(
            perm[...], bbuf[:, j].reshape(seq, LANES), preferred_element_type=f32
        )

    taps = [[jnp.broadcast_to(w_ref[j, i : i + 1, :], (CHUNKS, LANES)) for i in range(3)] for j in range(3)]
    decays = [table_row(0, m) for m in range(modes)]
    before = [
        [
            jnp.where(chunk_id == 0, 0.0, pltpu.roll(placed[j, (steps - i) * CHUNKS : (steps - i + 1) * CHUNKS, :], 1, 0))
            for j in range(3)
        ]
        for i in (1, 2)
    ]

    def first_pass(t, carry):
        one, two, state = carry
        at = pl.ds(pl.multiple_of(t * CHUNKS, CHUNKS), CHUNKS)
        now = [placed[j, at, :] for j in range(3)]
        feats = [taps[j][0] * now[j] + taps[j][1] * one[j] + taps[j][2] * two[j] for j in range(3)]
        product = feats[1] * feats[2]
        if isinstance(t, int):
            product = jnp.where(chunk_id == 0, 0.0, product)
        qbuf[at, :] = feats[0]
        pbuf[at, :] = product
        state = [decays[m] * state[m] + product for m in range(modes)]
        return now, one, state

    carry = (before[0], before[1], [jnp.zeros((CHUNKS, LANES), f32)] * modes)
    carry = first_pass(0, carry)
    carry = first_pass(1, carry)
    _, _, state = lax.fori_loop(2, steps, first_pass, carry, unroll=2)

    start = []
    for m in range(modes):
        total = state[m]
        for i, hop in enumerate(hops):
            total = total + table_row(6 + i, m) * jnp.where(chunk_id >= hop, pltpu.roll(total, hop, 0), 0.0)
        local[m : m + 1, :] = total[CHUNKS - 1 :, :]
        start.append(jnp.where(chunk_id >= 1, pltpu.roll(total, 1, 0), 0.0))
    for j in range(3):
        for i in range(2):
            local[modes + 2 * j + i : modes + 2 * j + i + 1, :] = placed[j, i * CHUNKS : i * CHUNKS + 1, :]
            at = (steps - 2 + i) * CHUNKS + CHUNKS - 1
            local[modes + 6 + 2 * j + i : modes + 7 + 2 * j + i, :] = placed[j, at : at + 1, :]
    local[modes + 12 :, :] = jnp.zeros((MESSAGE - modes - 12, LANES), f32)
    sent[...] = local[...].astype(jnp.bfloat16)

    def slab(shard):
        return met.at[pl.ds(pl.multiple_of((shard + 1) * MESSAGE, MESSAGE), MESSAGE)]

    def copy_c(shard):
        return pltpu.make_async_remote_copy(
            src_ref=sent,
            dst_ref=slab(s),
            send_sem=send_c.at[shard],
            recv_sem=recv_c.at[s],
            device_id={"ctx": shard},
            device_id_type=MESH,
        )

    @pl.loop(s + 1, n_ctx)
    def _(shard):
        copy_c(shard).start()

    met[pl.ds(pl.multiple_of((s + 1) * MESSAGE, MESSAGE), MESSAGE), :] = sent[...]

    gains = [table_row(1, m) for m in range(modes)]

    def second_pass(t, state):
        at = pl.ds(pl.multiple_of(t * CHUNKS, CHUNKS), CHUNKS)
        product = pbuf[at, :]
        state = [decays[m] * state[m] + product for m in range(modes)]
        terms = [gains[m] * state[m] for m in range(modes)]
        while len(terms) > 1:
            terms = [a + b for a, b in zip(terms[::2], terms[1::2])]
        ybuf[at, :] = terms[0]
        return state

    lax.fori_loop(0, steps, second_pass, start, unroll=2)

    @pl.loop(0, s)
    def _(shard):
        pltpu.make_async_copy(slab(shard), slab(shard), recv_c.at[shard]).wait()

    got[...] = met[...].astype(f32)

    def rim_products(pick_row):
        first, second = [], []
        for j in range(3):
            x0, x1 = pick_row(MESSAGE + modes + 2 * j), pick_row(MESSAGE + modes + 2 * j + 1)
            l0, l1 = pick_row(modes + 6 + 2 * j), pick_row(modes + 7 + 2 * j)
            tap = [w_ref[j, i : i + 1, :] for i in range(3)]
            first.append(tap[0] * x0 + tap[1] * l1 + tap[2] * l0)
            second.append(tap[0] * x1 + tap[1] * x0 + tap[2] * l1)
        return first[0], first[1] * first[2], second[0], second[1] * second[2]

    _, all0, _, all1 = rim_products(lambda i: got[pl.ds(i, n_ctx, stride=MESSAGE), :])
    here = got[pl.ds(pl.multiple_of(s * MESSAGE, MESSAGE), 2 * MESSAGE), :]
    q0, p0, q1, p1 = rim_products(lambda i: here[i : i + 1, :])

    entering = jnp.zeros((modes, LANES), f32)
    for shard in range(n_ctx - 1):
        ended = got[(shard + 1) * MESSAGE : (shard + 1) * MESSAGE + modes, :]
        ended = ended + table(4) * all0[shard : shard + 1, :] + table(5) * all1[shard : shard + 1, :]
        entering = entering + table(9 + shard) * ended
    entering = entering + table(2) * (p0 + table(2) * p1)
    early = jnp.sum(table(3), axis=0, keepdims=True) * p1

    pbuf[0:1, :] = p0
    qbuf[0:1, :] = q0
    pbuf[CHUNKS : CHUNKS + 1, :] = p1
    qbuf[CHUNKS : CHUNKS + 1, :] = q1
    ybuf[0:1, :] = ybuf[0:1, :] - early

    coming = [starts[m] * spread_row(entering, m) for m in range(modes)]
    direct = jnp.broadcast_to(pass_ref[...], (CHUNKS, LANES))

    def third_pass(t, coming):
        at = pl.ds(pl.multiple_of(t * CHUNKS, CHUNKS), CHUNKS)
        terms = coming
        while len(terms) > 1:
            terms = [a + b for a, b in zip(terms[::2], terms[1::2])]
        value = qbuf[at, :] * (ybuf[at, :] + terms[0] + direct * pbuf[at, :])
        tail[pl.ds(t, CHUNKS, stride=steps), :] = value
        return [decays[m] * coming[m] for m in range(modes)]

    lax.fori_loop(0, steps, third_pass, coming, unroll=2)
    out_ref[...] = tail[...].astype(out_ref.dtype)

    pltpu.make_async_copy(abuf.at[1:], abuf.at[1:], send_a).wait()
    pltpu.make_async_copy(abuf.at[group:], abuf.at[group:], send_b).wait()

    @pl.loop(s + 1, n_ctx)
    def _(shard):
        copy_c(shard).wait_send()


def shards(n_ctx, n_ch, records, rec_slot, short_w, residue, rate, passthrough):
    block, _, channels = records.shape
    modes = rate.shape[1]
    seq = n_ch * block
    f32 = jnp.float32
    vmem = pl.BlockSpec(memory_space=pltpu.VMEM)
    dma = pltpu.SemaphoreType.DMA
    return pl.pallas_call(
        functools.partial(kernel, n_ctx, n_ch, block, modes),
        out_shape=pltpu.VMEM((seq, LANES), jnp.bfloat16),
        in_specs=[pl.BlockSpec(memory_space=pl.ANY)] * 6,
        out_specs=vmem,
        scratch_shapes=[
            pltpu.VMEM((3, block, channels), jnp.bfloat16),
            pltpu.VMEM(rec_slot.shape, jnp.int32),
            pltpu.VMEM((3, 3, LANES), f32),
            pltpu.VMEM((modes, LANES), f32),
            pltpu.VMEM((modes, LANES), f32),
            pltpu.VMEM((1, LANES), f32),
            pltpu.VMEM((n_ch, 3, block, LANES), jnp.bfloat16),
            pltpu.VMEM((n_ch, 3, block, LANES), jnp.bfloat16),
            pltpu.VMEM((seq, seq), jnp.bfloat16),
            pltpu.VMEM((3, seq, LANES), f32),
            pltpu.VMEM((seq, LANES), f32),
            pltpu.VMEM((seq, LANES), f32),
            pltpu.VMEM((seq, LANES), f32),
            pltpu.VMEM((seq, LANES), f32),
            pltpu.VMEM((MESSAGE, LANES), f32),
            pltpu.VMEM((MESSAGE, LANES), jnp.bfloat16),
            pltpu.VMEM(((n_ctx + 1) * MESSAGE, LANES), jnp.bfloat16),
            pltpu.VMEM(((n_ctx + 1) * MESSAGE, LANES), f32),
            pltpu.VMEM((8 + n_ctx, modes, LANES), f32),
            pltpu.VMEM((modes, CHUNKS, LANES), f32),
            dma((6,)),
            dma,
            dma((n_ch,)),
            dma,
            dma,
            dma((n_ctx,)),
            dma((n_ctx,)),
            pltpu.SemaphoreType.REGULAR((n_ch,)),
            pltpu.SemaphoreType.REGULAR((n_ctx,)),
        ],
        compiler_params=pltpu.CompilerParams(
            collective_id=0, has_side_effects=True, vmem_limit_bytes=61 * 1024 * 1024
        ),
        name="hyena",
    )(
        records.transpose(1, 0, 2),
        rec_slot,
        short_w.transpose(0, 2, 1),
        residue.T,
        rate.T,
        passthrough[None, :],
    )


def solution(mesh):
    return jax.shard_map(
        functools.partial(shards, mesh.shape["ctx"], mesh.shape["ch"]),
        mesh=mesh,
        in_specs=(
            P(("ctx", "ch"), None, None),
            P(),
            P(None, "ch", None),
            P("ch", None),
            P("ch", None),
            P("ch"),
        ),
        out_specs=P("ctx", "ch"),
        check_vma=False,
    )
```

```python
import functools

import jax
import jax.numpy as jnp
from jax import lax
from jax.experimental import pallas as pl
from jax.experimental.pallas import tpu as pltpu
from jax.sharding import PartitionSpec as P

MESH = pl.DeviceIdType.MESH
LANES = 128
CHUNKS = 8
INNER = 4
CORES = 2
MESSAGE = 32


def near_first(count):
    return [(i + 1) // 2 if i % 2 else -(i // 2) for i in range(count)]


def rest(value, count):
    return value & (count - 1)


def times(value, count):
    return value >> (count.bit_length() - 1)


def kernel(
    n_ctx,
    n_ch,
    block,
    modes,
    x_hbm,
    slot_hbm,
    w_hbm,
    res_hbm,
    rate_hbm,
    pass_hbm,
    out_ref,
    x_ref,
    slot_ref,
    w_ref,
    res_ref,
    rate_ref,
    pass_ref,
    abuf,
    bbuf,
    perm,
    placed,
    pbuf,
    qbuf,
    ybuf,
    tail,
    local,
    sent,
    met,
    got,
    tables,
    starts,
    load,
    send_a,
    recv_a,
    send_b,
    recv_b,
    send_c,
    recv_c,
    ready_a,
    ready_b,
):
    s = lax.axis_index("ctx")
    c = lax.axis_index("ch")
    recs = n_ch
    group = recs // n_ctx
    seq = recs * block
    steps = seq // CHUNKS
    f32 = jnp.float32
    n_z, n_y = n_ch // INNER, n_ctx // CORES

    def place_of(ctx):
        y = times(ctx, CORES)
        return jnp.where(y == 0, 0, jnp.where(y <= n_y // 2, 2 * y - 1, 2 * (n_y - y))) * CORES + rest(ctx, CORES)

    def ctx_at(place):
        i = times(place, CORES)
        return jnp.where(rest(i, 2) == 1, times(i + 1, 2), rest(n_y - times(i, 2), n_y)) * CORES + rest(place, CORES)

    place = place_of(s)

    operands = [(slot_hbm, slot_ref), (w_hbm, w_ref), (res_hbm, res_ref), (rate_hbm, rate_ref), (pass_hbm, pass_ref)]
    fetches = [pltpu.make_async_copy(src, dst, load.at[i]) for i, (src, dst) in enumerate(operands)]

    barrier = pltpu.get_barrier_semaphore()

    @pl.loop(c + 1, n_ch)
    def _(ch):
        pl.semaphore_signal(barrier, inc=1, device_id={"ch": ch}, device_id_type=MESH)

    @pl.loop(place + 1, n_ctx)
    def _(p):
        pl.semaphore_signal(barrier, inc=1, device_id={"ctx": ctx_at(p)}, device_id_type=MESH)

    def block_of(ch, source=x_hbm):
        return source.at[:, :, pl.ds(pl.multiple_of(ch * LANES, LANES), LANES)]

    pltpu.make_async_copy(block_of(c), abuf.at[c], recv_a.at[c]).start()
    x_copy = pltpu.make_async_copy(x_hbm, x_ref, load.at[5])
    x_copy.start()
    for fetch in fetches:
        fetch.start()

    @pl.when(c + place > 0)
    def _():
        pl.semaphore_wait(barrier, c + place)

    def copy_a(ch, source=x_hbm):
        return pltpu.make_async_remote_copy(
            src_ref=block_of(ch, source),
            dst_ref=abuf.at[c],
            send_sem=send_a,
            recv_sem=recv_a.at[c],
            device_id={"ch": ch},
            device_id_type=MESH,
        )

    z, x = times(c, INNER), rest(c, INNER)
    offsets = [(dz, dx) for dz in near_first(n_z) for dx in range(INNER)][1:]
    for i in range(n_ch):
        ch = i // INNER * INNER + rest(x + i, INNER)

        @pl.when(ch < c)
        def _():
            pl.semaphore_signal(ready_a.at[c], inc=1, device_id={"ch": ch}, device_id_type=MESH)
            copy_a(ch).start()

    @pl.loop(0, place)
    def _(p):
        pl.semaphore_signal(ready_b.at[s], inc=1, device_id={"ctx": ctx_at(p)}, device_id_type=MESH)

    half = n_ch // 2

    def send_later(ch):
        pl.semaphore_wait(ready_a.at[ch], 1)
        copy_a(ch, x_ref).start()

    x_copy.wait()
    pl.loop(c + 1, jnp.where(c < half, half, n_ch))(send_later)

    for fetch in fetches:
        fetch.wait()
    col = lax.broadcasted_iota(jnp.int32, (recs, seq), 1)
    row = lax.broadcasted_iota(jnp.int32, (recs, seq), 0)
    pick = (row == (col // block) % group * n_ctx + s).astype(f32)
    spread = jnp.dot(slot_ref[...].astype(f32), pick, preferred_element_type=f32)
    col = lax.broadcasted_iota(jnp.int32, (n_ctx, seq), 1)
    row = lax.broadcasted_iota(jnp.int32, (n_ctx, seq), 0)
    spread = jnp.where(row == col // (block * group), spread, 0.0)
    target = jnp.sum(spread, axis=0, keepdims=True).astype(jnp.int32)
    target = target * block + lax.broadcasted_iota(jnp.int32, (1, seq), 1) % block
    target = target % steps * CHUNKS + target // steps

    rows_at_once = 16

    @pl.loop(0, seq // rows_at_once)
    def _(i):
        at = pl.multiple_of(i * rows_at_once, rows_at_once)
        here = lax.broadcasted_iota(jnp.int32, (rows_at_once, seq), 0) + at
        perm[pl.ds(at, rows_at_once), :] = jnp.where(here == target, 1.0, 0.0).astype(jnp.bfloat16)

    @pl.loop(s + 2, n_ctx + 1)
    def _(i):
        met[pl.ds(pl.multiple_of(i * MESSAGE, MESSAGE), MESSAGE), :] = jnp.zeros((MESSAGE, LANES), jnp.bfloat16)

    met[0:MESSAGE, :] = jnp.zeros((MESSAGE, LANES), jnp.bfloat16)

    chunk_id = lax.broadcasted_iota(jnp.int32, (CHUNKS, LANES), 0)

    def spread_row(table, m):
        return jnp.broadcast_to(table[m : m + 1, :], (CHUNKS, LANES))

    rate = rate_ref[...]
    gain = res_ref[...] * jnp.sqrt(2.0 * rate / modes)
    grow = jnp.exp(rate)
    hops = (1, 2, 4)
    named = [jnp.exp(-rate), gain, grow, gain * grow, jnp.exp(-rate * (seq - 1)), jnp.exp(-rate * (seq - 2))]
    named += [jnp.exp(-rate * (steps * hop)) for hop in hops]
    for shard in range(n_ctx - 1):
        behind = s - 1 - shard
        reach = jnp.exp(-rate * (seq * jnp.maximum(behind, 0)).astype(f32))
        named.append(jnp.where(behind >= 0, reach, 0.0))
    for i, table in enumerate(named):
        tables[i] = table
    since = (chunk_id * steps + 1).astype(f32)
    for m in range(modes):
        starts[m] = spread_row(gain, m) * jnp.exp(-spread_row(rate, m) * since)

    pl.loop(half, jnp.where(c < half, n_ch, half))(send_later)

    def forward(r):
        pltpu.make_async_copy(abuf.at[r], abuf.at[r], recv_a.at[r]).wait()
        owner, here = rest(r, n_ctx), s * group + times(r, n_ctx)

        @pl.when(owner != s)
        def _():
            pltpu.make_async_remote_copy(
                src_ref=abuf.at[r],
                dst_ref=bbuf.at[here],
                send_sem=send_b,
                recv_sem=recv_b,
                device_id={"ctx": owner},
                device_id_type=MESH,
            ).start()

        @pl.when(owner == s)
        def _():
            pltpu.make_async_copy(abuf.at[r], bbuf.at[here], recv_b).start()

    def first(r):
        @pl.when(place_of(r) > place)
        def _():
            pl.semaphore_wait(ready_b.at[r], 1)

        forward(r)

    @pl.when(c < n_ch // 2)
    def _():
        for dz, dx in offsets:
            r = rest(z - dz, n_z) * INNER + rest(x - dx, INNER)

            @pl.when((r < c) & (r < n_ctx))
            def _():
                first(r)

        @pl.loop(c, n_ctx)
        def _(r):
            first(r)

        for dz, dx in offsets:
            r = rest(z - dz, n_z) * INNER + rest(x - dx, INNER)

            @pl.when((r < c) & (r >= n_ctx))
            def _():
                forward(r)

        @pl.loop(jnp.maximum(c, n_ctx), n_ch)
        def _(r):
            forward(r)


    @pl.when(c >= n_ch // 2)
    def _():
        @pl.loop(0, n_ctx)
        def _(k):
            first(rest(s + n_ctx - 1 - k, n_ctx))

        @pl.loop(0, n_ctx)
        def _(k):
            forward(rest(s + n_ctx - 1 - k, n_ctx) + n_ctx)


    pltpu.make_async_copy(bbuf, bbuf, recv_b).wait()

    def table(i):
        return tables[i]

    def table_row(i, m):
        return jnp.broadcast_to(tables[i, m : m + 1, :], (CHUNKS, LANES))

    arrived = jnp.concatenate([bbuf[:, j].reshape(seq, LANES) for j in range(3)], axis=1)
    placed[...] = jnp.dot(perm[...], arrived, preferred_element_type=f32)

    def stream(j, start):
        return placed[pl.ds(start, CHUNKS), j * LANES : (j + 1) * LANES]

    taps = [[jnp.broadcast_to(w_ref[j, i : i + 1, :], (CHUNKS, LANES)) for i in range(3)] for j in range(3)]
    decays = [table_row(0, m) for m in range(modes)]
    before = [
        [
            jnp.where(chunk_id == 0, 0.0, pltpu.roll(stream(j, (steps - i) * CHUNKS), 1, 0))
            for j in range(3)
        ]
        for i in (1, 2)
    ]

    def first_pass(t, carry):
        one, two, state = carry
        at = pl.ds(pl.multiple_of(t * CHUNKS, CHUNKS), CHUNKS)
        now = [stream(j, pl.multiple_of(t * CHUNKS, CHUNKS)) for j in range(3)]
        feats = [taps[j][0] * now[j] + taps[j][1] * one[j] + taps[j][2] * two[j] for j in range(3)]
        product = feats[1] * feats[2]
        if isinstance(t, int):
            product = jnp.where(chunk_id == 0, 0.0, product)
        qbuf[at, :] = feats[0]
        pbuf[at, :] = product
        state = [decays[m] * state[m] + product for m in range(modes)]
        return now, one, state

    carry = (before[0], before[1], [jnp.zeros((CHUNKS, LANES), f32)] * modes)
    carry = first_pass(0, carry)
    carry = first_pass(1, carry)
    _, _, state = lax.fori_loop(2, steps, first_pass, carry, unroll=2)

    start = []
    for m in range(modes):
        total = state[m]
        for i, hop in enumerate(hops):
            total = total + table_row(6 + i, m) * jnp.where(chunk_id >= hop, pltpu.roll(total, hop, 0), 0.0)
        local[m : m + 1, :] = total[CHUNKS - 1 :, :]
        start.append(jnp.where(chunk_id >= 1, pltpu.roll(total, 1, 0), 0.0))
    for j in range(3):
        for i in range(2):
            local[modes + 2 * j + i : modes + 2 * j + i + 1, :] = placed[i * CHUNKS : i * CHUNKS + 1, j * LANES : (j + 1) * LANES]
            at = (steps - 2 + i) * CHUNKS + CHUNKS - 1
            local[modes + 6 + 2 * j + i : modes + 7 + 2 * j + i, :] = placed[at : at + 1, j * LANES : (j + 1) * LANES]
    local[modes + 12 :, :] = jnp.zeros((MESSAGE - modes - 12, LANES), f32)
    sent[...] = local[...].astype(jnp.bfloat16)

    def slab(shard):
        return met.at[pl.ds(pl.multiple_of((shard + 1) * MESSAGE, MESSAGE), MESSAGE)]

    def copy_c(shard):
        return pltpu.make_async_remote_copy(
            src_ref=sent,
            dst_ref=slab(s),
            send_sem=send_c.at[shard],
            recv_sem=recv_c.at[s],
            device_id={"ctx": shard},
            device_id_type=MESH,
        )

    @pl.loop(s + 1, n_ctx)
    def _(i):
        copy_c(s + n_ctx - i).start()

    met[pl.ds(pl.multiple_of((s + 1) * MESSAGE, MESSAGE), MESSAGE), :] = sent[...]

    gains = [table_row(1, m) for m in range(modes)]

    def second_pass(t, state):
        at = pl.ds(pl.multiple_of(t * CHUNKS, CHUNKS), CHUNKS)
        product = pbuf[at, :]
        state = [decays[m] * state[m] + product for m in range(modes)]
        terms = [gains[m] * state[m] for m in range(modes)]
        while len(terms) > 1:
            terms = [a + b for a, b in zip(terms[::2], terms[1::2])]
        ybuf[at, :] = terms[0]
        return state

    lax.fori_loop(0, steps, second_pass, start, unroll=2)

    @pl.loop(0, s)
    def _(shard):
        pltpu.make_async_copy(slab(shard), slab(shard), recv_c.at[shard]).wait()

    got[...] = met[...].astype(f32)

    def rim_products(pick_row):
        first, second = [], []
        for j in range(3):
            x0, x1 = pick_row(MESSAGE + modes + 2 * j), pick_row(MESSAGE + modes + 2 * j + 1)
            l0, l1 = pick_row(modes + 6 + 2 * j), pick_row(modes + 7 + 2 * j)
            tap = [w_ref[j, i : i + 1, :] for i in range(3)]
            first.append(tap[0] * x0 + tap[1] * l1 + tap[2] * l0)
            second.append(tap[0] * x1 + tap[1] * x0 + tap[2] * l1)
        return first[0], first[1] * first[2], second[0], second[1] * second[2]

    _, all0, _, all1 = rim_products(lambda i: got[pl.ds(i, n_ctx, stride=MESSAGE), :])
    here = got[pl.ds(pl.multiple_of(s * MESSAGE, MESSAGE), 2 * MESSAGE), :]
    q0, p0, q1, p1 = rim_products(lambda i: here[i : i + 1, :])

    entering = jnp.zeros((modes, LANES), f32)
    for shard in range(n_ctx - 1):
        ended = got[(shard + 1) * MESSAGE : (shard + 1) * MESSAGE + modes, :]
        ended = ended + table(4) * all0[shard : shard + 1, :] + table(5) * all1[shard : shard + 1, :]
        entering = entering + table(9 + shard) * ended
    entering = entering + table(2) * (p0 + table(2) * p1)
    early = jnp.sum(table(3), axis=0, keepdims=True) * p1

    pbuf[0:1, :] = p0
    qbuf[0:1, :] = q0
    pbuf[CHUNKS : CHUNKS + 1, :] = p1
    qbuf[CHUNKS : CHUNKS + 1, :] = q1
    ybuf[0:1, :] = ybuf[0:1, :] - early

    coming = [starts[m] * spread_row(entering, m) for m in range(modes)]
    direct = jnp.broadcast_to(pass_ref[...], (CHUNKS, LANES))

    def third_pass(t, coming):
        at = pl.ds(pl.multiple_of(t * CHUNKS, CHUNKS), CHUNKS)
        terms = coming
        while len(terms) > 1:
            terms = [a + b for a, b in zip(terms[::2], terms[1::2])]
        value = qbuf[at, :] * (ybuf[at, :] + terms[0] + direct * pbuf[at, :])
        tail[pl.ds(t, CHUNKS, stride=steps), :] = value
        return [decays[m] * coming[m] for m in range(modes)]

    lax.fori_loop(0, steps, third_pass, coming, unroll=2)
    out_ref[...] = tail[...].astype(out_ref.dtype)

    pltpu.make_async_copy(abuf.at[1:], abuf.at[1:], send_a).wait()
    pltpu.make_async_copy(abuf.at[group:], abuf.at[group:], send_b).wait()

    @pl.loop(s + 1, n_ctx)
    def _(shard):
        copy_c(shard).wait_send()


def shards(n_ctx, n_ch, records, rec_slot, short_w, residue, rate, passthrough):
    block, _, channels = records.shape
    modes = rate.shape[1]
    seq = n_ch * block
    f32 = jnp.float32
    vmem = pl.BlockSpec(memory_space=pltpu.VMEM)
    dma = pltpu.SemaphoreType.DMA
    return pl.pallas_call(
        functools.partial(kernel, n_ctx, n_ch, block, modes),
        out_shape=pltpu.VMEM((seq, LANES), jnp.bfloat16),
        in_specs=[pl.BlockSpec(memory_space=pl.ANY)] * 6,
        out_specs=vmem,
        scratch_shapes=[
            pltpu.VMEM((3, block, channels), jnp.bfloat16),
            pltpu.VMEM(rec_slot.shape, jnp.int32),
            pltpu.VMEM((3, 3, LANES), f32),
            pltpu.VMEM((modes, LANES), f32),
            pltpu.VMEM((modes, LANES), f32),
            pltpu.VMEM((1, LANES), f32),
            pltpu.VMEM((n_ch, 3, block, LANES), jnp.bfloat16),
            pltpu.VMEM((n_ch, 3, block, LANES), jnp.bfloat16),
            pltpu.VMEM((seq, seq), jnp.bfloat16),
            pltpu.VMEM((seq, 3 * LANES), f32),
            pltpu.VMEM((seq, LANES), f32),
            pltpu.VMEM((seq, LANES), f32),
            pltpu.VMEM((seq, LANES), f32),
            pltpu.VMEM((seq, LANES), f32),
            pltpu.VMEM((MESSAGE, LANES), f32),
            pltpu.VMEM((MESSAGE, LANES), jnp.bfloat16),
            pltpu.VMEM(((n_ctx + 1) * MESSAGE, LANES), jnp.bfloat16),
            pltpu.VMEM(((n_ctx + 1) * MESSAGE, LANES), f32),
            pltpu.VMEM((8 + n_ctx, modes, LANES), f32),
            pltpu.VMEM((modes, CHUNKS, LANES), f32),
            dma((6,)),
            dma,
            dma((n_ch,)),
            dma,
            dma,
            dma((n_ctx,)),
            dma((n_ctx,)),
            pltpu.SemaphoreType.REGULAR((n_ch,)),
            pltpu.SemaphoreType.REGULAR((n_ctx,)),
        ],
        compiler_params=pltpu.CompilerParams(
            collective_id=0, has_side_effects=True, vmem_limit_bytes=61 * 1024 * 1024
        ),
        name="hyena",
    )(
        records.transpose(1, 0, 2),
        rec_slot,
        short_w.transpose(0, 2, 1),
        residue.T,
        rate.T,
        passthrough[None, :],
    )


def solution(mesh):
    return jax.shard_map(
        functools.partial(shards, mesh.shape["ctx"], mesh.shape["ch"]),
        mesh=mesh,
        in_specs=(
            P(("ctx", "ch"), None, None),
            P(),
            P(None, "ch", None),
            P("ch", None),
            P("ch", None),
            P("ch"),
        ),
        out_specs=P("ctx", "ch"),
        check_vma=False,
    )
```

```python
import functools

import jax
import jax.numpy as jnp
from jax import lax
from jax.experimental import pallas as pl
from jax.experimental.pallas import tpu as pltpu
from jax.sharding import PartitionSpec as P

MESH = pl.DeviceIdType.MESH
LANES = 128
CHUNKS = 8
INNER = 4
CORES = 2
MESSAGE = 32


def near_first(count):
    return [(i + 1) // 2 if i % 2 else -(i // 2) for i in range(count)]


def rest(value, count):
    return value & (count - 1)


def times(value, count):
    return value >> (count.bit_length() - 1)


def kernel(
    n_ctx,
    n_ch,
    block,
    modes,
    x_hbm,
    slot_hbm,
    w_hbm,
    res_hbm,
    rate_hbm,
    pass_hbm,
    out_ref,
    x_ref,
    slot_ref,
    w_ref,
    res_ref,
    rate_ref,
    pass_ref,
    abuf,
    bbuf,
    perm,
    placed,
    pbuf,
    qbuf,
    ybuf,
    tail,
    local,
    sent,
    met,
    got,
    tables,
    starts,
    load,
    send_a,
    recv_a,
    send_b,
    recv_b,
    send_c,
    recv_c,
    ready_a,
    ready_b,
):
    s = lax.axis_index("ctx")
    c = lax.axis_index("ch")
    recs = n_ch
    group = recs // n_ctx
    seq = recs * block
    steps = seq // CHUNKS
    f32 = jnp.float32
    n_z, n_y = n_ch // INNER, n_ctx // CORES

    def place_of(ctx):
        y = times(ctx, CORES)
        return jnp.where(y == 0, 0, jnp.where(y <= n_y // 2, 2 * y - 1, 2 * (n_y - y))) * CORES + rest(ctx, CORES)

    def ctx_at(place):
        i = times(place, CORES)
        return jnp.where(rest(i, 2) == 1, times(i + 1, 2), rest(n_y - times(i, 2), n_y)) * CORES + rest(place, CORES)

    place = place_of(s)

    operands = [(slot_hbm, slot_ref), (w_hbm, w_ref), (res_hbm, res_ref), (rate_hbm, rate_ref), (pass_hbm, pass_ref)]
    fetches = [pltpu.make_async_copy(src, dst, load.at[i]) for i, (src, dst) in enumerate(operands)]

    barrier = pltpu.get_barrier_semaphore()

    @pl.loop(c + 1, n_ch)
    def _(ch):
        pl.semaphore_signal(barrier, inc=1, device_id={"ch": ch}, device_id_type=MESH)

    @pl.loop(place + 1, n_ctx)
    def _(p):
        pl.semaphore_signal(barrier, inc=1, device_id={"ctx": ctx_at(p)}, device_id_type=MESH)

    def block_of(ch, source=x_hbm):
        return source.at[:, :, pl.ds(pl.multiple_of(ch * LANES, LANES), LANES)]

    pltpu.make_async_copy(block_of(c), abuf.at[c], recv_a.at[c]).start()
    x_copy = pltpu.make_async_copy(x_hbm, x_ref, load.at[5])
    x_copy.start()
    for fetch in fetches:
        fetch.start()

    @pl.when(c + place > 0)
    def _():
        pl.semaphore_wait(barrier, c + place)

    def copy_a(ch, source=x_hbm):
        return pltpu.make_async_remote_copy(
            src_ref=block_of(ch, source),
            dst_ref=abuf.at[c],
            send_sem=send_a,
            recv_sem=recv_a.at[c],
            device_id={"ch": ch},
            device_id_type=MESH,
        )

    z, x = times(c, INNER), rest(c, INNER)
    offsets = [(dz, dx) for dz in near_first(n_z) for dx in range(INNER)][1:]
    for i in range(n_ch):
        ch = i // INNER * INNER + rest(x + i, INNER)

        @pl.when(ch < c)
        def _():
            pl.semaphore_signal(ready_a.at[c], inc=1, device_id={"ch": ch}, device_id_type=MESH)
            copy_a(ch).start()

    @pl.loop(0, place)
    def _(p):
        pl.semaphore_signal(ready_b.at[s], inc=1, device_id={"ctx": ctx_at(p)}, device_id_type=MESH)

    half = n_ch // 2

    def send_later(ch):
        pl.semaphore_wait(ready_a.at[ch], 1)
        copy_a(ch, x_ref).start()

    x_copy.wait()
    pl.loop(c + 1, jnp.where(c < half, half, n_ch))(send_later)

    for fetch in fetches:
        fetch.wait()
    col = lax.broadcasted_iota(jnp.int32, (recs, seq), 1)
    row = lax.broadcasted_iota(jnp.int32, (recs, seq), 0)
    pick = (row == (col // block) % group * n_ctx + s).astype(f32)
    spread = jnp.dot(slot_ref[...].astype(f32), pick, preferred_element_type=f32)
    col = lax.broadcasted_iota(jnp.int32, (n_ctx, seq), 1)
    row = lax.broadcasted_iota(jnp.int32, (n_ctx, seq), 0)
    spread = jnp.where(row == col // (block * group), spread, 0.0)
    target = jnp.sum(spread, axis=0, keepdims=True).astype(jnp.int32)
    target = target * block + lax.broadcasted_iota(jnp.int32, (1, seq), 1) % block
    target = target % steps * CHUNKS + target // steps

    rows_at_once = 16

    @pl.loop(0, seq // rows_at_once)
    def _(i):
        at = pl.multiple_of(i * rows_at_once, rows_at_once)
        here = lax.broadcasted_iota(jnp.int32, (rows_at_once, seq), 0) + at
        perm[pl.ds(at, rows_at_once), :] = jnp.where(here == target, 1.0, 0.0).astype(jnp.bfloat16)

    @pl.loop(s + 2, n_ctx + 1)
    def _(i):
        met[pl.ds(pl.multiple_of(i * MESSAGE, MESSAGE), MESSAGE), :] = jnp.zeros((MESSAGE, LANES), jnp.bfloat16)

    met[0:MESSAGE, :] = jnp.zeros((MESSAGE, LANES), jnp.bfloat16)

    chunk_id = lax.broadcasted_iota(jnp.int32, (CHUNKS, LANES), 0)

    def spread_row(table, m):
        return jnp.broadcast_to(table[m : m + 1, :], (CHUNKS, LANES))

    rate = rate_ref[...]
    gain = res_ref[...] * jnp.sqrt(2.0 * rate / modes)
    grow = jnp.exp(rate)
    hops = (1, 2, 4)
    named = [jnp.exp(-rate), gain, grow, gain * grow, jnp.exp(-rate * (seq - 1)), jnp.exp(-rate * (seq - 2))]
    named += [jnp.exp(-rate * (steps * hop)) for hop in hops]
    for shard in range(n_ctx - 1):
        behind = s - 1 - shard
        reach = jnp.exp(-rate * (seq * jnp.maximum(behind, 0)).astype(f32))
        named.append(jnp.where(behind >= 0, reach, 0.0))
    for i, table in enumerate(named):
        tables[i] = table
    since = (chunk_id * steps + 1).astype(f32)
    for m in range(modes):
        starts[m] = spread_row(gain, m) * jnp.exp(-spread_row(rate, m) * since)

    pl.loop(half, jnp.where(c < half, n_ch, half))(send_later)

    def forward(r):
        pltpu.make_async_copy(abuf.at[r], abuf.at[r], recv_a.at[r]).wait()
        owner, here = rest(r, n_ctx), s * group + times(r, n_ctx)

        @pl.when(owner != s)
        def _():
            pltpu.make_async_remote_copy(
                src_ref=abuf.at[r],
                dst_ref=bbuf.at[here],
                send_sem=send_b,
                recv_sem=recv_b,
                device_id={"ctx": owner},
                device_id_type=MESH,
            ).start()

        @pl.when(owner == s)
        def _():
            pltpu.make_async_copy(abuf.at[r], bbuf.at[here], recv_b).start()

    def first(r):
        owner = rest(r, n_ctx)

        @pl.when(place_of(owner) > place)
        def _():
            pl.semaphore_wait(ready_b.at[owner], 1)

        forward(r)

    @pl.when(c < n_ch // 2)
    def _():
        @pl.loop(0, n_ctx)
        def _(k):
            first(rest((z + times(k, INNER)) * INNER, n_ctx) + rest(k + s, INNER))

        @pl.loop(0, n_ctx)
        def _(k):
            forward(n_ctx + (k & -INNER) + rest(k + times(s, CORES), INNER))


    @pl.when(c >= n_ch // 2)
    def _():
        @pl.loop(0, n_ctx)
        def _(k):
            first(n_ctx + (k & -INNER) + rest(k + s, INNER))

        @pl.loop(0, n_ctx)
        def _(k):
            forward(rest(s + n_ctx - 1 - k, n_ctx))


    pltpu.make_async_copy(bbuf, bbuf, recv_b).wait()

    def table(i):
        return tables[i]

    def table_row(i, m):
        return jnp.broadcast_to(tables[i, m : m + 1, :], (CHUNKS, LANES))

    arrived = jnp.concatenate([bbuf[:, j].reshape(seq, LANES) for j in range(3)], axis=1)
    placed[...] = jnp.dot(perm[...], arrived, preferred_element_type=f32)

    def stream(j, start):
        return placed[pl.ds(start, CHUNKS), j * LANES : (j + 1) * LANES]

    taps = [[jnp.broadcast_to(w_ref[j, i : i + 1, :], (CHUNKS, LANES)) for i in range(3)] for j in range(3)]
    decays = [table_row(0, m) for m in range(modes)]
    before = [
        [
            jnp.where(chunk_id == 0, 0.0, pltpu.roll(stream(j, (steps - i) * CHUNKS), 1, 0))
            for j in range(3)
        ]
        for i in (1, 2)
    ]

    def first_pass(t, carry):
        one, two, state = carry
        at = pl.ds(pl.multiple_of(t * CHUNKS, CHUNKS), CHUNKS)
        now = [stream(j, pl.multiple_of(t * CHUNKS, CHUNKS)) for j in range(3)]
        feats = [taps[j][0] * now[j] + taps[j][1] * one[j] + taps[j][2] * two[j] for j in range(3)]
        product = feats[1] * feats[2]
        if isinstance(t, int):
            product = jnp.where(chunk_id == 0, 0.0, product)
        qbuf[at, :] = feats[0]
        pbuf[at, :] = product
        state = [decays[m] * state[m] + product for m in range(modes)]
        return now, one, state

    carry = (before[0], before[1], [jnp.zeros((CHUNKS, LANES), f32)] * modes)
    carry = first_pass(0, carry)
    carry = first_pass(1, carry)
    _, _, state = lax.fori_loop(2, steps, first_pass, carry, unroll=2)

    start = []
    for m in range(modes):
        total = state[m]
        for i, hop in enumerate(hops):
            total = total + table_row(6 + i, m) * jnp.where(chunk_id >= hop, pltpu.roll(total, hop, 0), 0.0)
        local[m : m + 1, :] = total[CHUNKS - 1 :, :]
        start.append(jnp.where(chunk_id >= 1, pltpu.roll(total, 1, 0), 0.0))
    for j in range(3):
        for i in range(2):
            local[modes + 2 * j + i : modes + 2 * j + i + 1, :] = placed[i * CHUNKS : i * CHUNKS + 1, j * LANES : (j + 1) * LANES]
            at = (steps - 2 + i) * CHUNKS + CHUNKS - 1
            local[modes + 6 + 2 * j + i : modes + 7 + 2 * j + i, :] = placed[at : at + 1, j * LANES : (j + 1) * LANES]
    local[modes + 12 :, :] = jnp.zeros((MESSAGE - modes - 12, LANES), f32)
    sent[...] = local[...].astype(jnp.bfloat16)

    def slab(shard):
        return met.at[pl.ds(pl.multiple_of((shard + 1) * MESSAGE, MESSAGE), MESSAGE)]

    def copy_c(shard):
        return pltpu.make_async_remote_copy(
            src_ref=sent,
            dst_ref=slab(s),
            send_sem=send_c.at[shard],
            recv_sem=recv_c.at[s],
            device_id={"ctx": shard},
            device_id_type=MESH,
        )

    @pl.loop(s + 1, n_ctx)
    def _(i):
        copy_c(s + n_ctx - i).start()

    met[pl.ds(pl.multiple_of((s + 1) * MESSAGE, MESSAGE), MESSAGE), :] = sent[...]

    gains = [table_row(1, m) for m in range(modes)]

    def second_pass(t, state):
        at = pl.ds(pl.multiple_of(t * CHUNKS, CHUNKS), CHUNKS)
        product = pbuf[at, :]
        state = [decays[m] * state[m] + product for m in range(modes)]
        terms = [gains[m] * state[m] for m in range(modes)]
        while len(terms) > 1:
            terms = [a + b for a, b in zip(terms[::2], terms[1::2])]
        ybuf[at, :] = terms[0]
        return state

    lax.fori_loop(0, steps, second_pass, start, unroll=2)

    @pl.loop(0, s)
    def _(shard):
        pltpu.make_async_copy(slab(shard), slab(shard), recv_c.at[shard]).wait()

    got[...] = met[...].astype(f32)

    def rim_products(pick_row):
        first, second = [], []
        for j in range(3):
            x0, x1 = pick_row(MESSAGE + modes + 2 * j), pick_row(MESSAGE + modes + 2 * j + 1)
            l0, l1 = pick_row(modes + 6 + 2 * j), pick_row(modes + 7 + 2 * j)
            tap = [w_ref[j, i : i + 1, :] for i in range(3)]
            first.append(tap[0] * x0 + tap[1] * l1 + tap[2] * l0)
            second.append(tap[0] * x1 + tap[1] * x0 + tap[2] * l1)
        return first[0], first[1] * first[2], second[0], second[1] * second[2]

    _, all0, _, all1 = rim_products(lambda i: got[pl.ds(i, n_ctx, stride=MESSAGE), :])
    here = got[pl.ds(pl.multiple_of(s * MESSAGE, MESSAGE), 2 * MESSAGE), :]
    q0, p0, q1, p1 = rim_products(lambda i: here[i : i + 1, :])

    entering = jnp.zeros((modes, LANES), f32)
    for shard in range(n_ctx - 1):
        ended = got[(shard + 1) * MESSAGE : (shard + 1) * MESSAGE + modes, :]
        ended = ended + table(4) * all0[shard : shard + 1, :] + table(5) * all1[shard : shard + 1, :]
        entering = entering + table(9 + shard) * ended
    entering = entering + table(2) * (p0 + table(2) * p1)
    early = jnp.sum(table(3), axis=0, keepdims=True) * p1

    pbuf[0:1, :] = p0
    qbuf[0:1, :] = q0
    pbuf[CHUNKS : CHUNKS + 1, :] = p1
    qbuf[CHUNKS : CHUNKS + 1, :] = q1
    ybuf[0:1, :] = ybuf[0:1, :] - early

    coming = [starts[m] * spread_row(entering, m) for m in range(modes)]
    direct = jnp.broadcast_to(pass_ref[...], (CHUNKS, LANES))

    def third_pass(t, coming):
        at = pl.ds(pl.multiple_of(t * CHUNKS, CHUNKS), CHUNKS)
        terms = coming
        while len(terms) > 1:
            terms = [a + b for a, b in zip(terms[::2], terms[1::2])]
        value = qbuf[at, :] * (ybuf[at, :] + terms[0] + direct * pbuf[at, :])
        tail[pl.ds(t, CHUNKS, stride=steps), :] = value
        return [decays[m] * coming[m] for m in range(modes)]

    lax.fori_loop(0, steps, third_pass, coming, unroll=2)
    out_ref[...] = tail[...].astype(out_ref.dtype)

    pltpu.make_async_copy(abuf.at[1:], abuf.at[1:], send_a).wait()
    pltpu.make_async_copy(abuf.at[group:], abuf.at[group:], send_b).wait()

    @pl.loop(s + 1, n_ctx)
    def _(shard):
        copy_c(shard).wait_send()


def shards(n_ctx, n_ch, records, rec_slot, short_w, residue, rate, passthrough):
    block, _, channels = records.shape
    modes = rate.shape[1]
    seq = n_ch * block
    f32 = jnp.float32
    vmem = pl.BlockSpec(memory_space=pltpu.VMEM)
    dma = pltpu.SemaphoreType.DMA
    return pl.pallas_call(
        functools.partial(kernel, n_ctx, n_ch, block, modes),
        out_shape=pltpu.VMEM((seq, LANES), jnp.bfloat16),
        in_specs=[pl.BlockSpec(memory_space=pl.ANY)] * 6,
        out_specs=vmem,
        scratch_shapes=[
            pltpu.VMEM((3, block, channels), jnp.bfloat16),
            pltpu.VMEM(rec_slot.shape, jnp.int32),
            pltpu.VMEM((3, 3, LANES), f32),
            pltpu.VMEM((modes, LANES), f32),
            pltpu.VMEM((modes, LANES), f32),
            pltpu.VMEM((1, LANES), f32),
            pltpu.VMEM((n_ch, 3, block, LANES), jnp.bfloat16),
            pltpu.VMEM((n_ch, 3, block, LANES), jnp.bfloat16),
            pltpu.VMEM((seq, seq), jnp.bfloat16),
            pltpu.VMEM((seq, 3 * LANES), f32),
            pltpu.VMEM((seq, LANES), f32),
            pltpu.VMEM((seq, LANES), f32),
            pltpu.VMEM((seq, LANES), f32),
            pltpu.VMEM((seq, LANES), f32),
            pltpu.VMEM((MESSAGE, LANES), f32),
            pltpu.VMEM((MESSAGE, LANES), jnp.bfloat16),
            pltpu.VMEM(((n_ctx + 1) * MESSAGE, LANES), jnp.bfloat16),
            pltpu.VMEM(((n_ctx + 1) * MESSAGE, LANES), f32),
            pltpu.VMEM((8 + n_ctx, modes, LANES), f32),
            pltpu.VMEM((modes, CHUNKS, LANES), f32),
            dma((6,)),
            dma,
            dma((n_ch,)),
            dma,
            dma,
            dma((n_ctx,)),
            dma((n_ctx,)),
            pltpu.SemaphoreType.REGULAR((n_ch,)),
            pltpu.SemaphoreType.REGULAR((n_ctx,)),
        ],
        compiler_params=pltpu.CompilerParams(
            collective_id=0, has_side_effects=True, vmem_limit_bytes=61 * 1024 * 1024
        ),
        name="hyena",
    )(
        records.transpose(1, 0, 2),
        rec_slot,
        short_w.transpose(0, 2, 1),
        residue.T,
        rate.T,
        passthrough[None, :],
    )


def solution(mesh):
    return jax.shard_map(
        functools.partial(shards, mesh.shape["ctx"], mesh.shape["ch"]),
        mesh=mesh,
        in_specs=(
            P(("ctx", "ch"), None, None),
            P(),
            P(None, "ch", None),
            P("ch", None),
            P("ch", None),
            P("ch"),
        ),
        out_specs=P("ctx", "ch"),
        check_vma=False,
    )
```

```python
import functools

import jax
import jax.numpy as jnp
from jax import lax
from jax.experimental import pallas as pl
from jax.experimental.pallas import tpu as pltpu
from jax.sharding import PartitionSpec as P

MESH = pl.DeviceIdType.MESH
LANES = 128
CHUNKS = 8
INNER = 4
CORES = 2
MESSAGE = 32


def near_first(count):
    return [(i + 1) // 2 if i % 2 else -(i // 2) for i in range(count)]


def rest(value, count):
    return value & (count - 1)


def times(value, count):
    return value >> (count.bit_length() - 1)


def kernel(
    n_ctx,
    n_ch,
    block,
    modes,
    x_hbm,
    slot_hbm,
    w_hbm,
    res_hbm,
    rate_hbm,
    pass_hbm,
    out_ref,
    x_ref,
    slot_ref,
    w_ref,
    res_ref,
    rate_ref,
    pass_ref,
    abuf,
    bbuf,
    perm,
    placed,
    pbuf,
    qbuf,
    ybuf,
    tail,
    local,
    sent,
    met,
    got,
    tables,
    starts,
    load,
    send_a,
    recv_a,
    send_b,
    recv_b,
    send_c,
    recv_c,
    ready_a,
    ready_b,
):
    s = lax.axis_index("ctx")
    c = lax.axis_index("ch")
    recs = n_ch
    group = recs // n_ctx
    seq = recs * block
    steps = seq // CHUNKS
    f32 = jnp.float32
    n_z, n_y = n_ch // INNER, n_ctx // CORES

    def place_of(ctx):
        y = times(ctx, CORES)
        return jnp.where(y == 0, 0, jnp.where(y <= n_y // 2, 2 * y - 1, 2 * (n_y - y))) * CORES + rest(ctx, CORES)

    def ctx_at(place):
        i = times(place, CORES)
        return jnp.where(rest(i, 2) == 1, times(i + 1, 2), rest(n_y - times(i, 2), n_y)) * CORES + rest(place, CORES)

    place = place_of(s)

    operands = [(slot_hbm, slot_ref), (w_hbm, w_ref), (res_hbm, res_ref), (rate_hbm, rate_ref), (pass_hbm, pass_ref)]
    fetches = [pltpu.make_async_copy(src, dst, load.at[i]) for i, (src, dst) in enumerate(operands)]

    barrier = pltpu.get_barrier_semaphore()

    @pl.loop(c + 1, n_ch)
    def _(ch):
        pl.semaphore_signal(barrier, inc=1, device_id={"ch": ch}, device_id_type=MESH)

    @pl.loop(place + 1, n_ctx)
    def _(p):
        pl.semaphore_signal(barrier, inc=1, device_id={"ctx": ctx_at(p)}, device_id_type=MESH)

    def block_of(ch, source=x_hbm):
        return source.at[:, :, pl.ds(pl.multiple_of(ch * LANES, LANES), LANES)]

    pltpu.make_async_copy(block_of(c), abuf.at[c], recv_a.at[c]).start()
    x_copy = pltpu.make_async_copy(x_hbm, x_ref, load.at[5])
    x_copy.start()
    for fetch in fetches:
        fetch.start()

    @pl.when(c + place > 0)
    def _():
        pl.semaphore_wait(barrier, c + place)

    def copy_a(ch, source=x_hbm):
        return pltpu.make_async_remote_copy(
            src_ref=block_of(ch, source),
            dst_ref=abuf.at[c],
            send_sem=send_a,
            recv_sem=recv_a.at[c],
            device_id={"ch": ch},
            device_id_type=MESH,
        )

    z, x = times(c, INNER), rest(c, INNER)
    offsets = [(dz, dx) for dz in near_first(n_z) for dx in range(INNER)][1:]
    for i in range(n_ch):
        ch = i // INNER * INNER + rest(x + i, INNER)

        @pl.when(ch < c)
        def _():
            pl.semaphore_signal(ready_a.at[c], inc=1, device_id={"ch": ch}, device_id_type=MESH)
            copy_a(ch).start()

    @pl.loop(0, place)
    def _(p):
        pl.semaphore_signal(ready_b.at[s], inc=1, device_id={"ctx": ctx_at(p)}, device_id_type=MESH)

    half = n_ch // 2

    def send_later(ch):
        pl.semaphore_wait(ready_a.at[ch], 1)
        copy_a(ch, x_ref).start()

    x_copy.wait()
    pl.loop(c + 1, jnp.where(c < half, half, n_ch))(send_later)

    for fetch in fetches:
        fetch.wait()
    col = lax.broadcasted_iota(jnp.int32, (recs, seq), 1)
    row = lax.broadcasted_iota(jnp.int32, (recs, seq), 0)
    pick = (row == (col // block) % group * n_ctx + s).astype(f32)
    spread = jnp.dot(slot_ref[...].astype(f32), pick, preferred_element_type=f32)
    col = lax.broadcasted_iota(jnp.int32, (n_ctx, seq), 1)
    row = lax.broadcasted_iota(jnp.int32, (n_ctx, seq), 0)
    spread = jnp.where(row == col // (block * group), spread, 0.0)
    target = jnp.sum(spread, axis=0, keepdims=True).astype(jnp.int32)
    target = target * block + lax.broadcasted_iota(jnp.int32, (1, seq), 1) % block
    target = target % steps * CHUNKS + target // steps

    rows_at_once = 16

    @pl.loop(0, seq // rows_at_once)
    def _(i):
        at = pl.multiple_of(i * rows_at_once, rows_at_once)
        here = lax.broadcasted_iota(jnp.int32, (rows_at_once, seq), 0) + at
        perm[pl.ds(at, rows_at_once), :] = jnp.where(here == target, 1.0, 0.0).astype(jnp.bfloat16)

    @pl.loop(s + 2, n_ctx + 1)
    def _(i):
        met[pl.ds(pl.multiple_of(i * MESSAGE, MESSAGE), MESSAGE), :] = jnp.zeros((MESSAGE, LANES), jnp.bfloat16)

    met[0:MESSAGE, :] = jnp.zeros((MESSAGE, LANES), jnp.bfloat16)

    chunk_id = lax.broadcasted_iota(jnp.int32, (CHUNKS, LANES), 0)

    def spread_row(table, m):
        return jnp.broadcast_to(table[m : m + 1, :], (CHUNKS, LANES))

    rate = rate_ref[...]
    gain = res_ref[...] * jnp.sqrt(2.0 * rate / modes)
    grow = jnp.exp(rate)
    hops = (1, 2, 4)
    named = [jnp.exp(-rate), gain, grow, gain * grow, jnp.exp(-rate * (seq - 1)), jnp.exp(-rate * (seq - 2))]
    named += [jnp.exp(-rate * (steps * hop)) for hop in hops]
    for shard in range(n_ctx - 1):
        behind = s - 1 - shard
        reach = jnp.exp(-rate * (seq * jnp.maximum(behind, 0)).astype(f32))
        named.append(jnp.where(behind >= 0, reach, 0.0))
    for i, table in enumerate(named):
        tables[i] = table
    since = (chunk_id * steps + 1).astype(f32)
    for m in range(modes):
        starts[m] = spread_row(gain, m) * jnp.exp(-spread_row(rate, m) * since)

    pl.loop(half, jnp.where(c < half, half + 2 * INNER, half))(send_later)

    def forward(r):
        pltpu.make_async_copy(abuf.at[r], abuf.at[r], recv_a.at[r]).wait()
        owner, here = rest(r, n_ctx), s * group + times(r, n_ctx)

        @pl.when(owner != s)
        def _():
            pltpu.make_async_remote_copy(
                src_ref=abuf.at[r],
                dst_ref=bbuf.at[here],
                send_sem=send_b,
                recv_sem=recv_b,
                device_id={"ctx": owner},
                device_id_type=MESH,
            ).start()

        @pl.when(owner == s)
        def _():
            pltpu.make_async_copy(abuf.at[r], bbuf.at[here], recv_b).start()

    def first(r):
        owner = rest(r, n_ctx)

        @pl.when(place_of(owner) > place)
        def _():
            pl.semaphore_wait(ready_b.at[owner], 1)

        forward(r)

    @pl.when(c < n_ch // 2)
    def _():
        @pl.loop(0, n_ctx)
        def _(k):
            first(rest((z + times(k, INNER)) * INNER, n_ctx) + rest(k + times(s, CORES), INNER))

        pl.loop(half + 2 * INNER, n_ch)(send_later)

        @pl.loop(0, n_ctx)
        def _(k):
            forward(n_ctx + (k & -INNER) + rest(k + times(s, CORES), INNER))


    @pl.when(c >= n_ch // 2)
    def _():
        @pl.loop(0, n_ctx)
        def _(k):
            first(n_ctx + (k & -INNER) + rest(k + s, INNER))

        @pl.loop(0, n_ctx)
        def _(k):
            forward(rest(s + n_ctx - 1 - k, n_ctx))


    pltpu.make_async_copy(bbuf, bbuf, recv_b).wait()

    def table(i):
        return tables[i]

    def table_row(i, m):
        return jnp.broadcast_to(tables[i, m : m + 1, :], (CHUNKS, LANES))

    arrived = jnp.concatenate([bbuf[:, j].reshape(seq, LANES) for j in range(3)], axis=1)
    placed[...] = jnp.dot(perm[...], arrived, preferred_element_type=f32)

    def stream(j, start):
        return placed[pl.ds(start, CHUNKS), j * LANES : (j + 1) * LANES]

    taps = [[jnp.broadcast_to(w_ref[j, i : i + 1, :], (CHUNKS, LANES)) for i in range(3)] for j in range(3)]
    decays = [table_row(0, m) for m in range(modes)]
    before = [
        [
            jnp.where(chunk_id == 0, 0.0, pltpu.roll(stream(j, (steps - i) * CHUNKS), 1, 0))
            for j in range(3)
        ]
        for i in (1, 2)
    ]

    def first_pass(t, carry):
        one, two, state = carry
        at = pl.ds(pl.multiple_of(t * CHUNKS, CHUNKS), CHUNKS)
        now = [stream(j, pl.multiple_of(t * CHUNKS, CHUNKS)) for j in range(3)]
        feats = [taps[j][0] * now[j] + taps[j][1] * one[j] + taps[j][2] * two[j] for j in range(3)]
        product = feats[1] * feats[2]
        if isinstance(t, int):
            product = jnp.where(chunk_id == 0, 0.0, product)
        qbuf[at, :] = feats[0]
        pbuf[at, :] = product
        state = [decays[m] * state[m] + product for m in range(modes)]
        return now, one, state

    carry = (before[0], before[1], [jnp.zeros((CHUNKS, LANES), f32)] * modes)
    carry = first_pass(0, carry)
    carry = first_pass(1, carry)
    _, _, state = lax.fori_loop(2, steps, first_pass, carry, unroll=2)

    start = []
    for m in range(modes):
        total = state[m]
        for i, hop in enumerate(hops):
            total = total + table_row(6 + i, m) * jnp.where(chunk_id >= hop, pltpu.roll(total, hop, 0), 0.0)
        local[m : m + 1, :] = total[CHUNKS - 1 :, :]
        start.append(jnp.where(chunk_id >= 1, pltpu.roll(total, 1, 0), 0.0))
    for j in range(3):
        for i in range(2):
            local[modes + 2 * j + i : modes + 2 * j + i + 1, :] = placed[i * CHUNKS : i * CHUNKS + 1, j * LANES : (j + 1) * LANES]
            at = (steps - 2 + i) * CHUNKS + CHUNKS - 1
            local[modes + 6 + 2 * j + i : modes + 7 + 2 * j + i, :] = placed[at : at + 1, j * LANES : (j + 1) * LANES]
    local[modes + 12 :, :] = jnp.zeros((MESSAGE - modes - 12, LANES), f32)
    sent[...] = local[...].astype(jnp.bfloat16)

    def slab(shard):
        return met.at[pl.ds(pl.multiple_of((shard + 1) * MESSAGE, MESSAGE), MESSAGE)]

    def copy_c(shard):
        return pltpu.make_async_remote_copy(
            src_ref=sent,
            dst_ref=slab(s),
            send_sem=send_c.at[shard],
            recv_sem=recv_c.at[s],
            device_id={"ctx": shard},
            device_id_type=MESH,
        )

    @pl.loop(s + 1, n_ctx)
    def _(i):
        copy_c(s + n_ctx - i).start()

    met[pl.ds(pl.multiple_of((s + 1) * MESSAGE, MESSAGE), MESSAGE), :] = sent[...]

    gains = [table_row(1, m) for m in range(modes)]

    def second_pass(t, state):
        at = pl.ds(pl.multiple_of(t * CHUNKS, CHUNKS), CHUNKS)
        product = pbuf[at, :]
        state = [decays[m] * state[m] + product for m in range(modes)]
        terms = [gains[m] * state[m] for m in range(modes)]
        while len(terms) > 1:
            terms = [a + b for a, b in zip(terms[::2], terms[1::2])]
        ybuf[at, :] = terms[0]
        return state

    lax.fori_loop(0, steps, second_pass, start, unroll=2)

    @pl.loop(0, s)
    def _(shard):
        pltpu.make_async_copy(slab(shard), slab(shard), recv_c.at[shard]).wait()

    got[...] = met[...].astype(f32)

    def rim_products(pick_row):
        first, second = [], []
        for j in range(3):
            x0, x1 = pick_row(MESSAGE + modes + 2 * j), pick_row(MESSAGE + modes + 2 * j + 1)
            l0, l1 = pick_row(modes + 6 + 2 * j), pick_row(modes + 7 + 2 * j)
            tap = [w_ref[j, i : i + 1, :] for i in range(3)]
            first.append(tap[0] * x0 + tap[1] * l1 + tap[2] * l0)
            second.append(tap[0] * x1 + tap[1] * x0 + tap[2] * l1)
        return first[0], first[1] * first[2], second[0], second[1] * second[2]

    _, all0, _, all1 = rim_products(lambda i: got[pl.ds(i, n_ctx, stride=MESSAGE), :])
    here = got[pl.ds(pl.multiple_of(s * MESSAGE, MESSAGE), 2 * MESSAGE), :]
    q0, p0, q1, p1 = rim_products(lambda i: here[i : i + 1, :])

    entering = jnp.zeros((modes, LANES), f32)
    for shard in range(n_ctx - 1):
        ended = got[(shard + 1) * MESSAGE : (shard + 1) * MESSAGE + modes, :]
        ended = ended + table(4) * all0[shard : shard + 1, :] + table(5) * all1[shard : shard + 1, :]
        entering = entering + table(9 + shard) * ended
    entering = entering + table(2) * (p0 + table(2) * p1)
    early = jnp.sum(table(3), axis=0, keepdims=True) * p1

    pbuf[0:1, :] = p0
    qbuf[0:1, :] = q0
    pbuf[CHUNKS : CHUNKS + 1, :] = p1
    qbuf[CHUNKS : CHUNKS + 1, :] = q1
    ybuf[0:1, :] = ybuf[0:1, :] - early

    coming = [starts[m] * spread_row(entering, m) for m in range(modes)]
    direct = jnp.broadcast_to(pass_ref[...], (CHUNKS, LANES))

    def third_pass(t, coming):
        at = pl.ds(pl.multiple_of(t * CHUNKS, CHUNKS), CHUNKS)
        terms = coming
        while len(terms) > 1:
            terms = [a + b for a, b in zip(terms[::2], terms[1::2])]
        value = qbuf[at, :] * (ybuf[at, :] + terms[0] + direct * pbuf[at, :])
        tail[pl.ds(t, CHUNKS, stride=steps), :] = value
        return [decays[m] * coming[m] for m in range(modes)]

    lax.fori_loop(0, steps, third_pass, coming, unroll=2)
    out_ref[...] = tail[...].astype(out_ref.dtype)

    pltpu.make_async_copy(abuf.at[1:], abuf.at[1:], send_a).wait()
    pltpu.make_async_copy(abuf.at[group:], abuf.at[group:], send_b).wait()

    @pl.loop(s + 1, n_ctx)
    def _(shard):
        copy_c(shard).wait_send()


def shards(n_ctx, n_ch, records, rec_slot, short_w, residue, rate, passthrough):
    block, _, channels = records.shape
    modes = rate.shape[1]
    seq = n_ch * block
    f32 = jnp.float32
    vmem = pl.BlockSpec(memory_space=pltpu.VMEM)
    dma = pltpu.SemaphoreType.DMA
    return pl.pallas_call(
        functools.partial(kernel, n_ctx, n_ch, block, modes),
        out_shape=pltpu.VMEM((seq, LANES), jnp.bfloat16),
        in_specs=[pl.BlockSpec(memory_space=pl.ANY)] * 6,
        out_specs=vmem,
        scratch_shapes=[
            pltpu.VMEM((3, block, channels), jnp.bfloat16),
            pltpu.VMEM(rec_slot.shape, jnp.int32),
            pltpu.VMEM((3, 3, LANES), f32),
            pltpu.VMEM((modes, LANES), f32),
            pltpu.VMEM((modes, LANES), f32),
            pltpu.VMEM((1, LANES), f32),
            pltpu.VMEM((n_ch, 3, block, LANES), jnp.bfloat16),
            pltpu.VMEM((n_ch, 3, block, LANES), jnp.bfloat16),
            pltpu.VMEM((seq, seq), jnp.bfloat16),
            pltpu.VMEM((seq, 3 * LANES), f32),
            pltpu.VMEM((seq, LANES), f32),
            pltpu.VMEM((seq, LANES), f32),
            pltpu.VMEM((seq, LANES), f32),
            pltpu.VMEM((seq, LANES), f32),
            pltpu.VMEM((MESSAGE, LANES), f32),
            pltpu.VMEM((MESSAGE, LANES), jnp.bfloat16),
            pltpu.VMEM(((n_ctx + 1) * MESSAGE, LANES), jnp.bfloat16),
            pltpu.VMEM(((n_ctx + 1) * MESSAGE, LANES), f32),
            pltpu.VMEM((8 + n_ctx, modes, LANES), f32),
            pltpu.VMEM((modes, CHUNKS, LANES), f32),
            dma((6,)),
            dma,
            dma((n_ch,)),
            dma,
            dma,
            dma((n_ctx,)),
            dma((n_ctx,)),
            pltpu.SemaphoreType.REGULAR((n_ch,)),
            pltpu.SemaphoreType.REGULAR((n_ctx,)),
        ],
        compiler_params=pltpu.CompilerParams(
            collective_id=0, has_side_effects=True, vmem_limit_bytes=61 * 1024 * 1024
        ),
        name="hyena",
    )(
        records.transpose(1, 0, 2),
        rec_slot,
        short_w.transpose(0, 2, 1),
        residue.T,
        rate.T,
        passthrough[None, :],
    )


def solution(mesh):
    return jax.shard_map(
        functools.partial(shards, mesh.shape["ctx"], mesh.shape["ch"]),
        mesh=mesh,
        in_specs=(
            P(("ctx", "ch"), None, None),
            P(),
            P(None, "ch", None),
            P("ch", None),
            P("ch", None),
            P("ch"),
        ),
        out_specs=P("ctx", "ch"),
        check_vma=False,
    )
```

```python
import functools

import jax
import jax.numpy as jnp
from jax import lax
from jax.experimental import pallas as pl
from jax.experimental.pallas import tpu as pltpu
from jax.sharding import PartitionSpec as P

MESH = pl.DeviceIdType.MESH
LANES = 128
CHUNKS = 8
INNER = 4
CORES = 2
MESSAGE = 32


def near_first(count):
    return [(i + 1) // 2 if i % 2 else -(i // 2) for i in range(count)]


def rest(value, count):
    return value & (count - 1)


def times(value, count):
    return value >> (count.bit_length() - 1)


def kernel(
    n_ctx,
    n_ch,
    block,
    modes,
    x_hbm,
    slot_hbm,
    w_hbm,
    res_hbm,
    rate_hbm,
    pass_hbm,
    out_ref,
    x_ref,
    slot_ref,
    w_ref,
    res_ref,
    rate_ref,
    pass_ref,
    abuf,
    bbuf,
    perm,
    placed,
    pbuf,
    qbuf,
    ybuf,
    local,
    sent,
    met,
    got,
    tables,
    starts,
    load,
    send_a,
    recv_a,
    send_b,
    recv_b,
    send_c,
    recv_c,
    ready_a,
    ready_b,
):
    s = lax.axis_index("ctx")
    c = lax.axis_index("ch")
    recs = n_ch
    group = recs // n_ctx
    seq = recs * block
    steps = seq // CHUNKS
    f32 = jnp.float32
    n_z, n_y = n_ch // INNER, n_ctx // CORES

    def place_of(ctx):
        y = times(ctx, CORES)
        return jnp.where(y == 0, 0, jnp.where(y <= n_y // 2, 2 * y - 1, 2 * (n_y - y))) * CORES + rest(ctx, CORES)

    def ctx_at(place):
        i = times(place, CORES)
        return jnp.where(rest(i, 2) == 1, times(i + 1, 2), rest(n_y - times(i, 2), n_y)) * CORES + rest(place, CORES)

    place = place_of(s)

    operands = [(slot_hbm, slot_ref), (w_hbm, w_ref), (res_hbm, res_ref), (rate_hbm, rate_ref), (pass_hbm, pass_ref)]
    fetches = [pltpu.make_async_copy(src, dst, load.at[i]) for i, (src, dst) in enumerate(operands)]

    barrier = pltpu.get_barrier_semaphore()

    @pl.loop(c + 1, n_ch)
    def _(ch):
        pl.semaphore_signal(barrier, inc=1, device_id={"ch": ch}, device_id_type=MESH)

    @pl.loop(place + 1, n_ctx)
    def _(p):
        pl.semaphore_signal(barrier, inc=1, device_id={"ctx": ctx_at(p)}, device_id_type=MESH)

    def block_of(ch, source=x_hbm):
        return source.at[:, :, pl.ds(pl.multiple_of(ch * LANES, LANES), LANES)]

    pltpu.make_async_copy(block_of(c), abuf.at[c], recv_a.at[c]).start()
    x_copy = pltpu.make_async_copy(x_hbm, x_ref, load.at[5])
    x_copy.start()
    for fetch in fetches:
        fetch.start()

    @pl.when(c + place > 0)
    def _():
        pl.semaphore_wait(barrier, c + place)

    def copy_a(ch, source=x_hbm):
        return pltpu.make_async_remote_copy(
            src_ref=block_of(ch, source),
            dst_ref=abuf.at[c],
            send_sem=send_a,
            recv_sem=recv_a.at[c],
            device_id={"ch": ch},
            device_id_type=MESH,
        )

    z, x = times(c, INNER), rest(c, INNER)
    offsets = [(dz, dx) for dz in near_first(n_z) for dx in range(INNER)][1:]
    for i in range(n_ch):
        ch = i // INNER * INNER + rest(x + i, INNER)

        @pl.when(ch < c)
        def _():
            pl.semaphore_signal(ready_a.at[c], inc=1, device_id={"ch": ch}, device_id_type=MESH)
            copy_a(ch).start()

    @pl.loop(0, place)
    def _(p):
        pl.semaphore_signal(ready_b.at[s], inc=1, device_id={"ctx": ctx_at(p)}, device_id_type=MESH)

    half = n_ch // 2

    def send_later(ch):
        pl.semaphore_wait(ready_a.at[ch], 1)
        copy_a(ch, x_ref).start()

    x_copy.wait()
    pl.loop(c + 1, jnp.where(c < half, half, n_ch))(send_later)

    for fetch in fetches:
        fetch.wait()
    col = lax.broadcasted_iota(jnp.int32, (recs, seq), 1)
    row = lax.broadcasted_iota(jnp.int32, (recs, seq), 0)
    pick = (row == (col // block) % group * n_ctx + s).astype(f32)
    spread = jnp.dot(slot_ref[...].astype(f32), pick, preferred_element_type=f32)
    col = lax.broadcasted_iota(jnp.int32, (n_ctx, seq), 1)
    row = lax.broadcasted_iota(jnp.int32, (n_ctx, seq), 0)
    spread = jnp.where(row == col // (block * group), spread, 0.0)
    target = jnp.sum(spread, axis=0, keepdims=True).astype(jnp.int32)
    target = target * block + lax.broadcasted_iota(jnp.int32, (1, seq), 1) % block
    target = target % steps * CHUNKS + target // steps

    rows_at_once = 16

    @pl.loop(0, seq // rows_at_once)
    def _(i):
        at = pl.multiple_of(i * rows_at_once, rows_at_once)
        here = lax.broadcasted_iota(jnp.int32, (rows_at_once, seq), 0) + at
        perm[pl.ds(at, rows_at_once), :] = jnp.where(here == target, 1.0, 0.0).astype(jnp.bfloat16)

    @pl.loop(s + 2, n_ctx + 1)
    def _(i):
        met[pl.ds(pl.multiple_of(i * MESSAGE, MESSAGE), MESSAGE), :] = jnp.zeros((MESSAGE, LANES), jnp.bfloat16)

    met[0:MESSAGE, :] = jnp.zeros((MESSAGE, LANES), jnp.bfloat16)

    chunk_id = lax.broadcasted_iota(jnp.int32, (CHUNKS, LANES), 0)

    def spread_row(table, m):
        return jnp.broadcast_to(table[m : m + 1, :], (CHUNKS, LANES))

    rate = rate_ref[...]
    gain = res_ref[...] * jnp.sqrt(2.0 * rate / modes)
    grow = jnp.exp(rate)
    hops = (1, 2, 4)
    named = [jnp.exp(-rate), gain, grow, gain * grow, jnp.exp(-rate * (seq - 1)), jnp.exp(-rate * (seq - 2))]
    named += [jnp.exp(-rate * (steps * hop)) for hop in hops]
    for shard in range(n_ctx - 1):
        behind = s - 1 - shard
        reach = jnp.exp(-rate * (seq * jnp.maximum(behind, 0)).astype(f32))
        named.append(jnp.where(behind >= 0, reach, 0.0))
    for i, table in enumerate(named):
        tables[i] = table
    since = (chunk_id * steps + 1).astype(f32)
    for m in range(modes):
        starts[m] = spread_row(gain, m) * jnp.exp(-spread_row(rate, m) * since)

    pl.loop(half, jnp.where(c < half, half + 2 * INNER, half))(send_later)

    def forward(r):
        pltpu.make_async_copy(abuf.at[r], abuf.at[r], recv_a.at[r]).wait()
        owner, here = rest(r, n_ctx), s * group + times(r, n_ctx)

        @pl.when(owner != s)
        def _():
            pltpu.make_async_remote_copy(
                src_ref=abuf.at[r],
                dst_ref=bbuf.at[here],
                send_sem=send_b,
                recv_sem=recv_b,
                device_id={"ctx": owner},
                device_id_type=MESH,
            ).start()

        @pl.when(owner == s)
        def _():
            pltpu.make_async_copy(abuf.at[r], bbuf.at[here], recv_b).start()

    def first(r):
        owner = rest(r, n_ctx)

        @pl.when(place_of(owner) > place)
        def _():
            pl.semaphore_wait(ready_b.at[owner], 1)

        forward(r)

    @pl.when(c < n_ch // 2)
    def _():
        @pl.loop(0, n_ctx)
        def _(k):
            first(rest((z + times(k, INNER)) * INNER, n_ctx) + rest(k + times(s, CORES), INNER))

        pl.loop(half + 2 * INNER, n_ch)(send_later)

        @pl.loop(0, n_ctx)
        def _(k):
            forward(n_ctx + (k & -INNER) + rest(k + times(s, CORES), INNER))


    @pl.when(c >= n_ch // 2)
    def _():
        @pl.loop(0, n_ctx)
        def _(k):
            first(n_ctx + (k & -INNER) + rest(k + s, INNER))

        @pl.loop(0, n_ctx)
        def _(k):
            forward(rest(s + n_ctx - 1 - k, n_ctx))


    pltpu.make_async_copy(bbuf, bbuf, recv_b).wait()

    def table(i):
        return tables[i]

    def table_row(i, m):
        return jnp.broadcast_to(tables[i, m : m + 1, :], (CHUNKS, LANES))

    arrived = jnp.concatenate([bbuf[:, j].reshape(seq, LANES) for j in range(3)], axis=1)
    placed[...] = jnp.dot(perm[...], arrived, preferred_element_type=f32)

    def stream(j, start):
        return placed[pl.ds(start, CHUNKS), j * LANES : (j + 1) * LANES]

    taps = [[jnp.broadcast_to(w_ref[j, i : i + 1, :], (CHUNKS, LANES)) for i in range(3)] for j in range(3)]
    decays = [table_row(0, m) for m in range(modes)]
    before = [
        [
            jnp.where(chunk_id == 0, 0.0, pltpu.roll(stream(j, (steps - i) * CHUNKS), 1, 0))
            for j in range(3)
        ]
        for i in (1, 2)
    ]

    def first_pass(t, carry):
        one, two, state = carry
        at = pl.ds(pl.multiple_of(t * CHUNKS, CHUNKS), CHUNKS)
        now = [stream(j, pl.multiple_of(t * CHUNKS, CHUNKS)) for j in range(3)]
        feats = [taps[j][0] * now[j] + taps[j][1] * one[j] + taps[j][2] * two[j] for j in range(3)]
        product = feats[1] * feats[2]
        if isinstance(t, int):
            product = jnp.where(chunk_id == 0, 0.0, product)
        qbuf[at, :] = feats[0]
        pbuf[at, :] = product
        state = [decays[m] * state[m] + product for m in range(modes)]
        return now, one, state

    carry = (before[0], before[1], [jnp.zeros((CHUNKS, LANES), f32)] * modes)
    carry = first_pass(0, carry)
    carry = first_pass(1, carry)
    _, _, state = lax.fori_loop(2, steps, first_pass, carry, unroll=2)

    start = []
    for m in range(modes):
        total = state[m]
        for i, hop in enumerate(hops):
            total = total + table_row(6 + i, m) * jnp.where(chunk_id >= hop, pltpu.roll(total, hop, 0), 0.0)
        local[m : m + 1, :] = total[CHUNKS - 1 :, :]
        start.append(jnp.where(chunk_id >= 1, pltpu.roll(total, 1, 0), 0.0))
    for j in range(3):
        for i in range(2):
            local[modes + 2 * j + i : modes + 2 * j + i + 1, :] = placed[i * CHUNKS : i * CHUNKS + 1, j * LANES : (j + 1) * LANES]
            at = (steps - 2 + i) * CHUNKS + CHUNKS - 1
            local[modes + 6 + 2 * j + i : modes + 7 + 2 * j + i, :] = placed[at : at + 1, j * LANES : (j + 1) * LANES]
    local[modes + 12 :, :] = jnp.zeros((MESSAGE - modes - 12, LANES), f32)
    sent[...] = local[...].astype(jnp.bfloat16)

    def slab(shard):
        return met.at[pl.ds(pl.multiple_of((shard + 1) * MESSAGE, MESSAGE), MESSAGE)]

    def copy_c(shard):
        return pltpu.make_async_remote_copy(
            src_ref=sent,
            dst_ref=slab(s),
            send_sem=send_c.at[shard],
            recv_sem=recv_c.at[s],
            device_id={"ctx": shard},
            device_id_type=MESH,
        )

    @pl.loop(s + 1, n_ctx)
    def _(i):
        copy_c(s + n_ctx - i).start()

    met[pl.ds(pl.multiple_of((s + 1) * MESSAGE, MESSAGE), MESSAGE), :] = sent[...]

    gains = [table_row(1, m) for m in range(modes)]

    def second_pass(t, state):
        at = pl.ds(pl.multiple_of(t * CHUNKS, CHUNKS), CHUNKS)
        product = pbuf[at, :]
        state = [decays[m] * state[m] + product for m in range(modes)]
        terms = [gains[m] * state[m] for m in range(modes)]
        while len(terms) > 1:
            terms = [a + b for a, b in zip(terms[::2], terms[1::2])]
        ybuf[at, :] = terms[0]
        return state

    lax.fori_loop(0, steps, second_pass, start, unroll=2)

    @pl.loop(0, s)
    def _(shard):
        pltpu.make_async_copy(slab(shard), slab(shard), recv_c.at[shard]).wait()

    got[...] = met[...].astype(f32)

    def rim_products(pick_row):
        first, second = [], []
        for j in range(3):
            x0, x1 = pick_row(MESSAGE + modes + 2 * j), pick_row(MESSAGE + modes + 2 * j + 1)
            l0, l1 = pick_row(modes + 6 + 2 * j), pick_row(modes + 7 + 2 * j)
            tap = [w_ref[j, i : i + 1, :] for i in range(3)]
            first.append(tap[0] * x0 + tap[1] * l1 + tap[2] * l0)
            second.append(tap[0] * x1 + tap[1] * x0 + tap[2] * l1)
        return first[0], first[1] * first[2], second[0], second[1] * second[2]

    _, all0, _, all1 = rim_products(lambda i: got[pl.ds(i, n_ctx, stride=MESSAGE), :])
    here = got[pl.ds(pl.multiple_of(s * MESSAGE, MESSAGE), 2 * MESSAGE), :]
    q0, p0, q1, p1 = rim_products(lambda i: here[i : i + 1, :])

    entering = jnp.zeros((modes, LANES), f32)
    for shard in range(n_ctx - 1):
        ended = got[(shard + 1) * MESSAGE : (shard + 1) * MESSAGE + modes, :]
        ended = ended + table(4) * all0[shard : shard + 1, :] + table(5) * all1[shard : shard + 1, :]
        entering = entering + table(9 + shard) * ended
    entering = entering + table(2) * (p0 + table(2) * p1)
    early = jnp.sum(table(3), axis=0, keepdims=True) * p1

    pbuf[0:1, :] = p0
    qbuf[0:1, :] = q0
    pbuf[CHUNKS : CHUNKS + 1, :] = p1
    qbuf[CHUNKS : CHUNKS + 1, :] = q1
    ybuf[0:1, :] = ybuf[0:1, :] - early

    coming = [starts[m] * spread_row(entering, m) for m in range(modes)]
    direct = jnp.broadcast_to(pass_ref[...], (CHUNKS, LANES))

    def third_pass(t, coming):
        at = pl.ds(pl.multiple_of(t * CHUNKS, CHUNKS), CHUNKS)
        terms = coming
        while len(terms) > 1:
            terms = [a + b for a, b in zip(terms[::2], terms[1::2])]
        value = qbuf[at, :] * (ybuf[at, :] + terms[0] + direct * pbuf[at, :])
        out_ref[pl.ds(t, CHUNKS, stride=steps), :] = value
        return [decays[m] * coming[m] for m in range(modes)]

    lax.fori_loop(0, steps, third_pass, coming, unroll=2)

    pltpu.make_async_copy(abuf.at[1:], abuf.at[1:], send_a).wait()
    pltpu.make_async_copy(abuf.at[group:], abuf.at[group:], send_b).wait()

    @pl.loop(s + 1, n_ctx)
    def _(shard):
        copy_c(shard).wait_send()


def shards(n_ctx, n_ch, records, rec_slot, short_w, residue, rate, passthrough):
    block, _, channels = records.shape
    modes = rate.shape[1]
    seq = n_ch * block
    f32 = jnp.float32
    vmem = pl.BlockSpec(memory_space=pltpu.VMEM)
    dma = pltpu.SemaphoreType.DMA
    return pl.pallas_call(
        functools.partial(kernel, n_ctx, n_ch, block, modes),
        out_shape=pltpu.VMEM((seq, LANES), f32),
        in_specs=[pl.BlockSpec(memory_space=pl.ANY)] * 6,
        out_specs=vmem,
        scratch_shapes=[
            pltpu.VMEM((3, block, channels), jnp.bfloat16),
            pltpu.VMEM(rec_slot.shape, jnp.int32),
            pltpu.VMEM((3, 3, LANES), f32),
            pltpu.VMEM((modes, LANES), f32),
            pltpu.VMEM((modes, LANES), f32),
            pltpu.VMEM((1, LANES), f32),
            pltpu.VMEM((n_ch, 3, block, LANES), jnp.bfloat16),
            pltpu.VMEM((n_ch, 3, block, LANES), jnp.bfloat16),
            pltpu.VMEM((seq, seq), jnp.bfloat16),
            pltpu.VMEM((seq, 3 * LANES), f32),
            pltpu.VMEM((seq, LANES), f32),
            pltpu.VMEM((seq, LANES), f32),
            pltpu.VMEM((seq, LANES), f32),
            pltpu.VMEM((MESSAGE, LANES), f32),
            pltpu.VMEM((MESSAGE, LANES), jnp.bfloat16),
            pltpu.VMEM(((n_ctx + 1) * MESSAGE, LANES), jnp.bfloat16),
            pltpu.VMEM(((n_ctx + 1) * MESSAGE, LANES), f32),
            pltpu.VMEM((8 + n_ctx, modes, LANES), f32),
            pltpu.VMEM((modes, CHUNKS, LANES), f32),
            dma((6,)),
            dma,
            dma((n_ch,)),
            dma,
            dma,
            dma((n_ctx,)),
            dma((n_ctx,)),
            pltpu.SemaphoreType.REGULAR((n_ch,)),
            pltpu.SemaphoreType.REGULAR((n_ctx,)),
        ],
        compiler_params=pltpu.CompilerParams(
            collective_id=0, has_side_effects=True, vmem_limit_bytes=61 * 1024 * 1024
        ),
        name="hyena",
    )(
        records.transpose(1, 0, 2),
        rec_slot,
        short_w.transpose(0, 2, 1),
        residue.T,
        rate.T,
        passthrough[None, :],
    ).astype(jnp.bfloat16)


def solution(mesh):
    return jax.shard_map(
        functools.partial(shards, mesh.shape["ctx"], mesh.shape["ch"]),
        mesh=mesh,
        in_specs=(
            P(("ctx", "ch"), None, None),
            P(),
            P(None, "ch", None),
            P("ch", None),
            P("ch", None),
            P("ch"),
        ),
        out_specs=P("ctx", "ch"),
        check_vma=False,
    )
```
